512 devices in a mesh: tm: 16 (over y_hi, x, core), rows: 32 (over y_lo, z).
Axes of the slice: x: 4, y: 4 (y_hi: 2, y_lo: 2; y = y_hi * 2 + y_lo), z: 16, core: 2. Of those that a mesh axis runs over, the one named last changes fastest.
Arguments:
- features: bfloat16 [64, 96, 128, 128], P('tm', None, 'rows'), may hold values from -6 to 6
- weights: bfloat16 [3, 3, 3, 96, 96], replicated, may hold values from -0.125 to 0.125
- cotangent: bfloat16 [64, 96, 128, 128], P('tm', None, 'rows'), may hold values from -6 to 6
Outputs:
- input_grad: bfloat16 [64, 96, 128, 128], P('tm', None, 'rows')
- weight_grad: float32 [3, 3, 3, 96, 96], replicated
The draws below stay inside these ranges and needn't reach their ends.
All inputs are finite; a program needn't handle non-finite values.
Results may differ from the reference program's by a relative error of at most 0.004.
Values may be sent and summed in bfloat16 or wider, within the bound.
No kernel may reach another device: no remote copies, remote signals or barrier semaphores. Data moves between devices by JAX's collectives and lax.ppermute only.
A program may use at most 64 MiB of HBM per device.

```python
import jax
import jax.numpy as jnp
from jax import lax

CH = 96
W = 128
FRAMES = 64
HEIGHT = 128


def shard_levels(own_key, extent, cuts, low, largest):
    def one(dim, shards_of):
        draws = jax.random.uniform(jax.random.fold_in(jax.random.fold_in(own_key, 6), dim), (shards_of,), jnp.float32, low / len(cuts), largest / len(cuts))
        return jnp.repeat(jnp.exp(draws), extent[dim] // shards_of).reshape((-1,) + (1,) * (len(extent) - dim - 1))

    gain = one(*cuts[0])
    for cut in cuts[1:]:
        gain = gain * one(*cut)
    return gain


def centred(stream_key, shape, scale, limit, cuts=(), kind=jnp.bfloat16):
    factor_of = shard_levels(stream_key, shape, cuts, -0.22, 0.18) if cuts else 1.0
    entries = jax.random.normal(stream_key, shape, jnp.float32) * scale * factor_of
    return jnp.minimum(jnp.maximum(entries, -limit), limit).astype(kind)


def setup_inputs(seed: int = 0) -> dict:
    key_of = jax.random.split(jax.random.key(seed), 4)
    return {
        "features": centred(key_of[0], (FRAMES, CH, HEIGHT, W), 1.0, 6.0, ((0, 16), (2, 32))),
        "weights": centred(key_of[1], (3, 3, 3, CH, CH), (27 * CH) ** -0.5, 0.125),
        "cotangent": centred(key_of[2], (FRAMES, CH, HEIGHT, W), 1.0, 6.0, ((0, 16), (2, 32))),
    }


def normalize(features):
    values = features.astype(jnp.float32)
    scale = lax.rsqrt(lax.optimization_barrier(jnp.mean(values * values, axis=1, keepdims=True)) + 1e-06)
    return (values * scale, scale)

def reference(features, weights, cotangent):
    normed, scale = normalize(features)
    active = jax.nn.silu(normed).astype(jnp.bfloat16)
    frames, _, height, width = features.shape
    act_pad = jnp.pad(active, ((2, 0), (0, 0), (1, 1), (1, 1))).astype(jnp.float32)
    grad_pad = jnp.pad(cotangent, ((0, 2), (0, 0), (1, 1), (1, 1))).astype(jnp.float32)
    grad_plain = cotangent.astype(jnp.float32)
    active_grad = jnp.zeros(normed.shape, jnp.float32)
    pieces = []
    for time_tap in range(3):
        for row_tap in range(3):
            for col_tap in range(3):
                kernel = weights[time_tap, row_tap, col_tap].astype(jnp.float32)
                window = grad_pad[2 - time_tap:2 - time_tap + frames, :, 2 - row_tap:2 - row_tap + height, 2 - col_tap:2 - col_tap + width]
                active_grad = active_grad + jnp.einsum('oc,fohw->fchw', kernel, window)
                source = act_pad[time_tap:time_tap + frames, :, row_tap:row_tap + height, col_tap:col_tap + width]
                pieces.append(jnp.einsum('fohw,fchw->oc', grad_plain, source))
    weight_grad = jnp.stack(pieces).reshape(weights.shape) * (1.0 / jnp.sqrt(jnp.float32(frames * height * width)))
    sigma = jax.nn.sigmoid(normed)
    normed_grad = active_grad * sigma * (1.0 + normed * (1.0 - sigma))
    inner = lax.optimization_barrier(jnp.mean(normed_grad * normed, axis=1, keepdims=True))
    input_grad = scale * (normed_grad - normed * inner) + grad_plain
    return (input_grad.astype(jnp.bfloat16), weight_grad)
```

```python
import jax
import jax.numpy as jnp
from jax import lax
from jax.experimental import pallas as pl
from jax.experimental.pallas import tpu as pltpu
from jax.sharding import Mesh, PartitionSpec as P

TM = ("y_hi", "x", "core")
ROWS = ("y_lo", "z")
PLANE = ("y_hi", "x", "core", "y_lo")
CH = 96
W = 128
F = 4
H = 4
FE = F + 2
HE = H + 2
PACKED = 2048
F32 = jnp.float32
BF16 = jnp.bfloat16


def dot(a, b, dims):
    return lax.dot_general(a, b, (dims, ((), ())), preferred_element_type=F32)


def row_picker(h):
    pair = lax.broadcasted_iota(jnp.int32, (CH, H * CH), 1)
    channel = lax.broadcasted_iota(jnp.int32, (CH, H * CH), 0)
    return jnp.where(pair == channel * H + h, 1.0, 0.0).astype(BF16)


def row_placer(h):
    pair = lax.broadcasted_iota(jnp.int32, (H * CH, CH), 0)
    channel = lax.broadcasted_iota(jnp.int32, (H * CH, CH), 1)
    return jnp.where(pair == channel * H + h, 1.0, 0.0).astype(BF16)


def compute_kernel(feat, cot, next_frames, above, below, weights, grad_out, packed, win, act, normed, sigma, scale, wsum):
    lane = lax.broadcasted_iota(jnp.int32, (CH, W), 1)

    cot_all = jnp.concatenate([cot[f] for f in range(F)] + [next_frames[f] for f in range(2)], axis=1)
    feat_all = jnp.concatenate([feat[f] for f in range(F)], axis=1)
    for row in range(HE):
        if row == 0:
            plain = jnp.concatenate([above[f] for f in range(FE)], axis=1).astype(F32)
        elif row == HE - 1:
            plain = jnp.concatenate([below[f] for f in range(FE)], axis=1).astype(F32)
        else:
            plain = dot(row_picker(row - 1), cot_all, ((1,), (0,)))
        base = row * 3 * CH
        win[base + CH : base + 2 * CH, :] = plain.astype(BF16)
        for f in range(FE):
            part = plain[:, f * W : (f + 1) * W]
            left = jnp.where(lane == W - 1, 0.0, pltpu.roll(part, W - 1, 1))
            right = jnp.where(lane == 0, 0.0, pltpu.roll(part, 1, 1))
            win[base : base + CH, f * W : (f + 1) * W] = left.astype(BF16)
            win[base + 2 * CH : base + 3 * CH, f * W : (f + 1) * W] = right.astype(BF16)

    for h in range(H):
        values = dot(row_picker(h), feat_all, ((1,), (0,)))
        s = lax.rsqrt(jnp.sum(values * values, axis=0, keepdims=True) * (1.0 / CH) + 1e-06)
        n = values * s
        sig = 1.0 / (1.0 + jnp.exp(-n))
        act[h] = (n * sig).astype(BF16)
        normed[h] = n
        sigma[h] = sig
        scale[h] = s

    for t in range(3):
        total = None
        for h in range(H):
            window = win[h * 3 * CH : (h + 3) * 3 * CH, (2 - t) * W : (2 - t) * W + F * W]
            term = dot(window, act[h], ((1,), (1,)))
            total = term if total is None else total + term
        wsum[t * 9 * CH : (t + 1) * 9 * CH, :] = total

    third = CH // 3
    for group in range(6):
        last = wsum[(group * 4 + 3) * CH : (group * 4 + 4) * CH, :]
        for k in range(3):
            own = wsum[(group * 4 + k) * CH : (group * 4 + k + 1) * CH, :]
            tile = jnp.concatenate([own, last[:, k * third : (k + 1) * third]], axis=1)
            packed[(group * 3 + k) * CH : (group * 3 + k + 1) * CH, :] = tile.astype(BF16)
    for k in range(3):
        own = wsum[(24 + k) * CH : (25 + k) * CH, :]
        tile = jnp.concatenate([own, jnp.zeros((CH, W - CH), F32)], axis=1)
        packed[(18 + k) * CH : (19 + k) * CH, :] = tile.astype(BF16)
    packed[21 * CH :, :] = jnp.zeros((PACKED - 21 * CH, W), BF16)

    by_time = []
    for t in range(3):
        stacked = jnp.concatenate([weights[t * 9 + r * 3 + c] for r in (2, 1, 0) for c in range(3)], axis=0)
        by_time.append(stacked.T)
    placed = None
    for h in range(H):
        grad = None
        for t in range(3):
            window = win[h * 3 * CH : (h + 3) * 3 * CH, (2 - t) * W : (2 - t) * W + F * W]
            term = dot(by_time[t], window, ((1,), (0,)))
            grad = term if grad is None else grad + term
        n, sig = normed[h], sigma[h]
        grad = grad * sig * (1.0 + n * (1.0 - sig))
        inner = jnp.sum(grad * n, axis=0, keepdims=True) * (1.0 / CH)
        own = win[(h + 1) * 3 * CH + CH : (h + 1) * 3 * CH + 2 * CH, : F * W].astype(F32)
        result = (scale[h] * (grad - n * inner) + own).astype(BF16)
        term = dot(row_placer(h), result, ((1,), (0,)))
        placed = term if placed is None else placed + term
    for f in range(F):
        grad_out[f] = placed[:, f * W : (f + 1) * W].astype(BF16)


def unpack_kernel(norm_factor, packed, out):
    third = CH // 3

    def place(position, value):
        t, k, c = position // 9, position // 3 % 3, position % 3
        out[t * 9 + (2 - k) * 3 + c] = value * norm_factor

    for group in range(6):
        tiles = [packed[(group * 3 + k) * CH : (group * 3 + k + 1) * CH, :].astype(F32) for k in range(3)]
        for k in range(3):
            place(group * 4 + k, tiles[k][:, :CH])
        place(group * 4 + 3, jnp.concatenate([tile[:, CH:] for tile in tiles], axis=1))
    for k in range(3):
        place(24 + k, packed[(18 + k) * CH : (19 + k) * CH, :].astype(F32)[:, :CH])


def vmem(count):
    return [pl.BlockSpec(memory_space=pltpu.VMEM)] * count


def spread(value, count):
    return jnp.broadcast_to(value, (count,) + value.shape)


def local(features, weights, cotangent):
    tm, rows = lax.axis_size(TM), lax.axis_size(ROWS)
    plane, depth = lax.axis_size(PLANE), lax.axis_size("z")
    cells = F * tm * H * rows * W

    next_frames = lax.ppermute(cotangent[:2], TM, [(i + 1, i) for i in range(tm - 1)])
    ext = jnp.concatenate([cotangent, next_frames], axis=0)
    above = lax.ppermute(ext[:, :, H - 1, :], ROWS, [(i, i + 1) for i in range(rows - 1)])
    below = lax.ppermute(ext[:, :, 0, :], ROWS, [(i + 1, i) for i in range(rows - 1)])

    input_grad, packed = pl.pallas_call(
        compute_kernel,
        out_shape=(
            jax.ShapeDtypeStruct((F, CH * H, W), BF16),
            jax.ShapeDtypeStruct((PACKED, W), BF16),
        ),
        in_specs=vmem(6),
        out_specs=tuple(vmem(2)),
        scratch_shapes=[
            pltpu.VMEM((HE * 3 * CH, FE * W), BF16),
            pltpu.VMEM((H, CH, F * W), BF16),
            pltpu.VMEM((H, CH, F * W), F32),
            pltpu.VMEM((H, CH, F * W), F32),
            pltpu.VMEM((H, 1, F * W), F32),
            pltpu.VMEM((27 * CH, CH), F32),
        ],
        compiler_params=pltpu.CompilerParams(vmem_limit_bytes=40 << 20),
        name="compute",
    )(
        features.reshape(F, CH * H, W),
        cotangent.reshape(F, CH * H, W),
        next_frames.reshape(2, CH * H, W),
        above,
        below,
        weights.reshape(27, CH, CH),
    )

    part = PACKED // plane
    parts = lax.all_to_all(packed.reshape(plane, part, W), PLANE, 0, 0)
    mine = jnp.sum(parts.astype(F32), axis=0).astype(BF16)
    slabs = lax.all_to_all(spread(mine, depth), "z", 0, 0)
    mine = jnp.sum(slabs.astype(F32), axis=0).astype(BF16)
    whole = lax.all_to_all(spread(mine, plane), PLANE, 0, 0).reshape(PACKED, W)

    weight_grad = pl.pallas_call(
        lambda *refs: unpack_kernel(1.0 / float(cells) ** 0.5, *refs),
        out_shape=jax.ShapeDtypeStruct((27, CH, CH), F32),
        in_specs=vmem(1),
        out_specs=vmem(1)[0],
        compiler_params=pltpu.CompilerParams(vmem_limit_bytes=40 << 20),
        name="unpack",
    )(whole)
    return (input_grad.reshape(F, CH, H, W), weight_grad.reshape(3, 3, 3, CH, CH))


def solution(mesh):
    fine = Mesh(mesh.devices.reshape(2, 4, 2, 2, 16), ("y_hi", "x", "core", "y_lo", "z"))
    return jax.shard_map(
        local,
        mesh=fine,
        in_specs=(P(TM, None, ROWS, None), P(), P(TM, None, ROWS, None)),
        out_specs=(P(TM, None, ROWS, None), P()),
        check_vma=False,
    )
```

```python
import jax
import jax.numpy as jnp
from jax import lax
from jax.experimental import pallas as pl
from jax.experimental.pallas import tpu as pltpu
from jax.sharding import Mesh, PartitionSpec as P

TM = ("y_hi", "x", "core")
ROWS = ("y_lo", "z_pair", "z_in")
PLANE = ("y_hi", "x", "core", "y_lo", "z_in")
CH = 96
W = 128
F = 4
H = 4
FE = F + 2
HE = H + 2
PACKED = 2048
F32 = jnp.float32
BF16 = jnp.bfloat16


def dot(a, b, dims):
    return lax.dot_general(a, b, (dims, ((), ())), preferred_element_type=F32)


def row_picker(h):
    pair = lax.broadcasted_iota(jnp.int32, (CH, H * CH), 1)
    channel = lax.broadcasted_iota(jnp.int32, (CH, H * CH), 0)
    return jnp.where(pair == channel * H + h, 1.0, 0.0).astype(BF16)


def row_placer(h):
    pair = lax.broadcasted_iota(jnp.int32, (H * CH, CH), 0)
    channel = lax.broadcasted_iota(jnp.int32, (H * CH, CH), 1)
    return jnp.where(pair == channel * H + h, 1.0, 0.0).astype(BF16)


def compute_kernel(feat, cot, next_frames, above, below, weights, grad_out, packed, win, act, normed, sigma, scale, wsum):
    lane = lax.broadcasted_iota(jnp.int32, (CH, W), 1)

    cot_all = jnp.concatenate([cot[f] for f in range(F)] + [next_frames[f] for f in range(2)], axis=1)
    feat_all = jnp.concatenate([feat[f] for f in range(F)], axis=1)
    for row in range(HE):
        if row == 0:
            plain = jnp.concatenate([above[f] for f in range(FE)], axis=1).astype(F32)
        elif row == HE - 1:
            plain = jnp.concatenate([below[f] for f in range(FE)], axis=1).astype(F32)
        else:
            plain = dot(row_picker(row - 1), cot_all, ((1,), (0,)))
        base = row * 3 * CH
        win[base + CH : base + 2 * CH, :] = plain.astype(BF16)
        for f in range(FE):
            part = plain[:, f * W : (f + 1) * W]
            left = jnp.where(lane == W - 1, 0.0, pltpu.roll(part, W - 1, 1))
            right = jnp.where(lane == 0, 0.0, pltpu.roll(part, 1, 1))
            win[base : base + CH, f * W : (f + 1) * W] = left.astype(BF16)
            win[base + 2 * CH : base + 3 * CH, f * W : (f + 1) * W] = right.astype(BF16)

    for h in range(H):
        values = dot(row_picker(h), feat_all, ((1,), (0,)))
        s = lax.rsqrt(jnp.sum(values * values, axis=0, keepdims=True) * (1.0 / CH) + 1e-06)
        n = values * s
        sig = 1.0 / (1.0 + jnp.exp(-n))
        act[h] = (n * sig).astype(BF16)
        normed[h] = n
        sigma[h] = sig
        scale[h] = s

    for t in range(3):
        total = None
        for h in range(H):
            window = win[h * 3 * CH : (h + 3) * 3 * CH, (2 - t) * W : (2 - t) * W + F * W]
            term = dot(window, act[h], ((1,), (1,)))
            total = term if total is None else total + term
        wsum[t * 9 * CH : (t + 1) * 9 * CH, :] = total

    third = CH // 3
    for group in range(6):
        last = wsum[(group * 4 + 3) * CH : (group * 4 + 4) * CH, :]
        for k in range(3):
            own = wsum[(group * 4 + k) * CH : (group * 4 + k + 1) * CH, :]
            tile = jnp.concatenate([own, last[:, k * third : (k + 1) * third]], axis=1)
            packed[(group * 3 + k) * CH : (group * 3 + k + 1) * CH, :] = tile.astype(BF16)
    for k in range(3):
        own = wsum[(24 + k) * CH : (25 + k) * CH, :]
        tile = jnp.concatenate([own, jnp.zeros((CH, W - CH), F32)], axis=1)
        packed[(18 + k) * CH : (19 + k) * CH, :] = tile.astype(BF16)
    packed[21 * CH :, :] = jnp.zeros((PACKED - 21 * CH, W), BF16)

    by_time = []
    for t in range(3):
        stacked = jnp.concatenate([weights[t * 9 + r * 3 + c] for r in (2, 1, 0) for c in range(3)], axis=0)
        by_time.append(stacked.T)
    placed = None
    for h in range(H):
        grad = None
        for t in range(3):
            window = win[h * 3 * CH : (h + 3) * 3 * CH, (2 - t) * W : (2 - t) * W + F * W]
            term = dot(by_time[t], window, ((1,), (0,)))
            grad = term if grad is None else grad + term
        n, sig = normed[h], sigma[h]
        grad = grad * sig * (1.0 + n * (1.0 - sig))
        inner = jnp.sum(grad * n, axis=0, keepdims=True) * (1.0 / CH)
        own = win[(h + 1) * 3 * CH + CH : (h + 1) * 3 * CH + 2 * CH, : F * W].astype(F32)
        result = (scale[h] * (grad - n * inner) + own).astype(BF16)
        term = dot(row_placer(h), result, ((1,), (0,)))
        placed = term if placed is None else placed + term
    for f in range(F):
        grad_out[f] = placed[:, f * W : (f + 1) * W].astype(BF16)


def unpack_kernel(norm_factor, packed, out):
    third = CH // 3

    def place(position, value):
        t, k, c = position // 9, position // 3 % 3, position % 3
        out[t * 9 + (2 - k) * 3 + c] = value * norm_factor

    for group in range(6):
        tiles = [packed[(group * 3 + k) * CH : (group * 3 + k + 1) * CH, :].astype(F32) for k in range(3)]
        for k in range(3):
            place(group * 4 + k, tiles[k][:, :CH])
        place(group * 4 + 3, jnp.concatenate([tile[:, CH:] for tile in tiles], axis=1))
    for k in range(3):
        place(24 + k, packed[(18 + k) * CH : (19 + k) * CH, :].astype(F32)[:, :CH])


def vmem(count):
    return [pl.BlockSpec(memory_space=pltpu.VMEM)] * count


def spread(value, count):
    return jnp.broadcast_to(value, (count,) + value.shape)


def local(features, weights, cotangent):
    tm, rows = lax.axis_size(TM), lax.axis_size(ROWS)
    plane, depth = lax.axis_size(PLANE), lax.axis_size("z_pair")
    cells = F * tm * H * rows * W

    next_frames = lax.ppermute(cotangent[:2], TM, [(i + 1, i) for i in range(tm - 1)])
    ext = jnp.concatenate([cotangent, next_frames], axis=0)
    above = lax.ppermute(ext[:, :, H - 1, :], ROWS, [(i, i + 1) for i in range(rows - 1)])
    below = lax.ppermute(ext[:, :, 0, :], ROWS, [(i + 1, i) for i in range(rows - 1)])

    input_grad, packed = pl.pallas_call(
        compute_kernel,
        out_shape=(
            jax.ShapeDtypeStruct((F, CH * H, W), BF16),
            jax.ShapeDtypeStruct((PACKED, W), BF16),
        ),
        in_specs=vmem(6),
        out_specs=tuple(vmem(2)),
        scratch_shapes=[
            pltpu.VMEM((HE * 3 * CH, FE * W), BF16),
            pltpu.VMEM((H, CH, F * W), BF16),
            pltpu.VMEM((H, CH, F * W), F32),
            pltpu.VMEM((H, CH, F * W), F32),
            pltpu.VMEM((H, 1, F * W), F32),
            pltpu.VMEM((27 * CH, CH), F32),
        ],
        compiler_params=pltpu.CompilerParams(vmem_limit_bytes=40 << 20),
        name="compute",
    )(
        features.reshape(F, CH * H, W),
        cotangent.reshape(F, CH * H, W),
        next_frames.reshape(2, CH * H, W),
        above,
        below,
        weights.reshape(27, CH, CH),
    )

    part = PACKED // plane
    parts = lax.all_to_all(packed.reshape(plane, part, W), PLANE, 0, 0)
    mine = jnp.sum(parts.astype(F32), axis=0).astype(BF16)
    slabs = lax.all_to_all(spread(mine, depth), "z_pair", 0, 0)
    mine = jnp.sum(slabs.astype(F32), axis=0).astype(BF16)
    whole = lax.all_to_all(spread(mine, plane), PLANE, 0, 0).reshape(PACKED, W)

    weight_grad = pl.pallas_call(
        lambda *refs: unpack_kernel(1.0 / float(cells) ** 0.5, *refs),
        out_shape=jax.ShapeDtypeStruct((27, CH, CH), F32),
        in_specs=vmem(1),
        out_specs=vmem(1)[0],
        compiler_params=pltpu.CompilerParams(vmem_limit_bytes=40 << 20),
        name="unpack",
    )(whole)
    return (input_grad.reshape(F, CH, H, W), weight_grad.reshape(3, 3, 3, CH, CH))


def solution(mesh):
    fine = Mesh(mesh.devices.reshape(2, 4, 2, 2, 8, 2), ("y_hi", "x", "core", "y_lo", "z_pair", "z_in"))
    return jax.shard_map(
        local,
        mesh=fine,
        in_specs=(P(TM, None, ROWS, None), P(), P(TM, None, ROWS, None)),
        out_specs=(P(TM, None, ROWS, None), P()),
        check_vma=False,
    )
```

```python
import jax
import jax.numpy as jnp
from jax import lax
from jax.experimental import pallas as pl
from jax.experimental.pallas import tpu as pltpu
from jax.sharding import Mesh, PartitionSpec as P

TM = ("y_hi", "x", "core")
ROWS = ("y_lo", "z_pair", "z_in")
PLANE = ("y_hi", "x", "core", "y_lo", "z_in")
CH = 96
W = 128
F = 4
H = 4
FW = F * W
NEXT = 2 * W
TAP = 3 * CH
PACKED = 2048
F32 = jnp.float32
BF16 = jnp.bfloat16


def dot(a, b, contract):
    return lax.dot_general(a, b, (contract, ((), ())), preferred_element_type=F32)


def row_major():
    parts = []
    for h in range(H):
        pair = lax.broadcasted_iota(jnp.int32, (CH, H * CH), 1)
        channel = lax.broadcasted_iota(jnp.int32, (CH, H * CH), 0)
        parts.append(jnp.where(pair == channel * H + h, 1.0, 0.0).astype(BF16))
    return jnp.concatenate(parts, axis=0)


def frames(ref, count):
    return jnp.concatenate([ref[f] for f in range(count)], axis=1)


def shifted(value, step):
    lane = lax.broadcasted_iota(jnp.int32, (CH, W), 1)
    parts = []
    for f in range(value.shape[1] // W):
        part = pltpu.roll(value[:, f * W : (f + 1) * W], (-step) % W, 1)
        parts.append(jnp.where(lane == (W - 1 if step > 0 else 0), 0.0, part))
    return jnp.concatenate(parts, axis=1)


def own_kernel(feat, cot, weights, own, act, normed, slope, scale, by_out):
    order = row_major()
    own[...] = dot(order, frames(cot, F), ((1,), (0,))).astype(BF16)
    values = dot(order, frames(feat, F), ((1,), (0,)))
    for h in range(H):
        x = values[h * CH : (h + 1) * CH]
        s = lax.rsqrt(jnp.sum(x * x, axis=0, keepdims=True) * (1.0 / CH) + 1e-06)
        n = x * s
        sigma = 1.0 / (1.0 + jnp.exp(-n))
        a = (n * sigma).astype(BF16).astype(F32)
        act[h, :CH] = shifted(a, -1).astype(BF16)
        act[h, CH : 2 * CH] = a.astype(BF16)
        act[h, 2 * CH :] = shifted(a, 1).astype(BF16)
        normed[h] = n
        slope[h] = sigma * (1.0 + n * (1.0 - sigma))
        scale[h] = s
    stacked = [
        jnp.concatenate([weights[t * 9 + (2 - k) * 3 + c].astype(F32) for c in range(3)], axis=1)
        for t in range(3)
        for k in range(3)
    ]
    by_out[...] = jnp.concatenate(stacked, axis=0).T.astype(BF16)


def next_kernel(cot, own, after, bottom, top):
    after[...] = dot(row_major(), frames(cot, 2), ((1,), (0,))).astype(BF16)
    for h, out in ((H - 1, bottom), (0, top)):
        out[:, :FW] = own[h * CH : (h + 1) * CH, :]
        out[:, FW:] = after[h * CH : (h + 1) * CH, :]


def row_gradients(h, mine, later, act, normed, slope, scale, by_out):
    windows = [
        jnp.concatenate([mine[:, (2 - t) * W :], later[:, : (2 - t) * W]], axis=1) if t < 2 else mine for t in range(3)
    ]
    terms = [dot(windows[t], act[h], ((1,), (1,))) for t in range(3)]
    products = dot(by_out[...], jnp.concatenate(windows, axis=0), ((1,), (0,)))
    grad = products[CH : 2 * CH] + shifted(products[:CH], 1) + shifted(products[2 * CH :], -1)
    n = normed[h]
    grad = grad * slope[h]
    inner = jnp.sum(grad * n, axis=0, keepdims=True) * (1.0 / CH)
    result = scale[h] * (grad - n * inner) + mine[CH : 2 * CH].astype(F32)
    return terms, result.astype(BF16)


def inner_kernel(own, after, act, normed, slope, scale, by_out, wsum, result):
    total = None
    for h in (1, 2):
        rows = slice((h - 1) * CH, (h + 2) * CH)
        terms, result[h - 1] = row_gradients(h, own[rows], after[rows], act, normed, slope, scale, by_out)
        total = terms if total is None else [a + b for a, b in zip(total, terms)]
    for t in range(3):
        wsum[t] = total[t]


def edge_kernel(above, below, own, after, act, normed, slope, scale, by_out, wsum, result, grad_out, packed):
    args = (act, normed, slope, scale, by_out)
    mine = jnp.concatenate([above[:, :FW], own[: 2 * CH]], axis=0)
    later = jnp.concatenate([above[:, FW:], after[: 2 * CH]], axis=0)
    first, first_row = row_gradients(0, mine, later, *args)
    mine = jnp.concatenate([own[2 * CH :], below[:, :FW]], axis=0)
    later = jnp.concatenate([after[2 * CH :], below[:, FW:]], axis=0)
    last, last_row = row_gradients(H - 1, mine, later, *args)

    rests = []
    for t in range(3):
        total = wsum[t] + first[t] + last[t]
        for j in range(2):
            packed[(2 * t + j) * TAP : (2 * t + j + 1) * TAP, :] = total[:, j * W : (j + 1) * W].astype(BF16)
        rests.append(total[:, 2 * W :])
    rests.append(jnp.zeros((TAP, W - CH), F32))
    packed[6 * TAP : 7 * TAP, :] = jnp.concatenate(rests, axis=1).astype(BF16)
    packed[7 * TAP :, :] = jnp.zeros((PACKED - 7 * TAP, W), BF16)

    rows = jnp.concatenate([first_row, result[0], result[1], last_row], axis=0)
    placed = dot(row_major().astype(F32).T.astype(BF16), rows, ((1,), (0,)))
    for f in range(F):
        grad_out[f] = placed[:, f * W : (f + 1) * W].astype(BF16)


def unpack_kernel(norm_factor, packed, out):
    rests = packed[6 * TAP : 7 * TAP, :].astype(F32)
    width = TAP - 2 * W
    for t in range(3):
        tiles = [packed[(2 * t + j) * TAP : (2 * t + j + 1) * TAP, :].astype(F32) for j in range(2)]
        block = jnp.concatenate(tiles + [rests[:, t * width : (t + 1) * width]], axis=1) * norm_factor
        for c in range(3):
            column = block[:, c * CH : (c + 1) * CH]
            for k in range(3):
                out[t * 9 + (2 - k) * 3 + c] = column[k * CH : (k + 1) * CH]


def call(kernel, name, outs, args, flops=0):
    place = pl.BlockSpec(memory_space=pltpu.VMEM)
    return pl.pallas_call(
        kernel,
        out_shape=tuple(jax.ShapeDtypeStruct(shape, dtype) for shape, dtype in outs),
        in_specs=[place] * len(args),
        out_specs=(place,) * len(outs),
        compiler_params=pltpu.CompilerParams(vmem_limit_bytes=32 << 20),
        cost_estimate=pl.CostEstimate(flops=flops, bytes_accessed=4 << 20, transcendentals=0),
        name=name,
    )(*args)


def spread(value, count):
    return jnp.broadcast_to(value, (count,) + value.shape)


def local(features, weights, cotangent):
    tm, rows = lax.axis_size(TM), lax.axis_size(ROWS)
    plane, depth = lax.axis_size(PLANE), lax.axis_size("z_pair")
    cells = F * tm * H * rows * W
    features = features.reshape(F, CH * H, W)
    cotangent = cotangent.reshape(F, CH * H, W)

    next_frames = lax.ppermute(cotangent[:2], TM, [(i + 1, i) for i in range(tm - 1)])
    own, *local_values = call(
        own_kernel,
        "own",
        [
            ((H * CH, FW), BF16),
            ((H, TAP, FW), BF16),
            ((H, CH, FW), F32),
            ((H, CH, FW), F32),
            ((H, 1, FW), F32),
            ((TAP, 3 * TAP), BF16),
        ],
        (features, cotangent, weights.reshape(27, CH, CH)),
        1 << 31,
    )
    after, bottom, top = call(
        next_kernel,
        "next_frames",
        [((H * CH, NEXT), BF16), ((CH, FW + NEXT), BF16), ((CH, FW + NEXT), BF16)],
        (next_frames, own),
    )
    above = lax.ppermute(bottom, ROWS, [(i, i + 1) for i in range(rows - 1)])
    below = lax.ppermute(top, ROWS, [(i + 1, i) for i in range(rows - 1)])
    wsum, result = call(
        inner_kernel,
        "inner_rows",
        [((3, TAP, TAP), F32), ((2, CH, FW), BF16)],
        (own, after, *local_values),
        1 << 31,
    )
    input_grad, packed = call(
        edge_kernel,
        "edge_rows",
        [((F, CH * H, W), BF16), ((PACKED, W), BF16)],
        (above, below, own, after, *local_values, wsum, result),
        1 << 31,
    )

    part = PACKED // plane
    parts = lax.all_to_all(packed.reshape(plane, part, W), PLANE, 0, 0)
    mine = jnp.sum(parts.astype(F32), axis=0).astype(BF16)
    slabs = lax.all_to_all(spread(mine, depth), "z_pair", 0, 0)
    mine = jnp.sum(slabs.astype(F32), axis=0).astype(BF16)
    whole = lax.all_to_all(spread(mine, plane), PLANE, 0, 0).reshape(PACKED, W)

    (weight_grad,) = call(
        lambda *refs: unpack_kernel(1.0 / float(cells) ** 0.5, *refs),
        "unpack",
        [((27, CH, CH), F32)],
        (whole,),
    )
    return (input_grad.reshape(F, CH, H, W), weight_grad.reshape(3, 3, 3, CH, CH))


def solution(mesh):
    fine = Mesh(
        mesh.devices.reshape(2, 4, 2, 2, 8, 2), ("y_hi", "x", "core", "y_lo", "z_pair", "z_in")
    )
    return jax.shard_map(
        local,
        mesh=fine,
        in_specs=(P(TM, None, ROWS, None), P(), P(TM, None, ROWS, None)),
        out_specs=(P(TM, None, ROWS, None), P()),
        check_vma=False,
    )
```

```python
import jax
import jax.numpy as jnp
from jax import lax
from jax.experimental import pallas as pl
from jax.experimental.pallas import tpu as pltpu
from jax.sharding import Mesh, PartitionSpec as P

TM = ("y_hi", "x", "core")
ROWS = ("y_lo", "z_pair", "z_in")
PLANE = ("y_hi", "x", "core", "y_lo", "z_in")
CH = 96
W = 128
F = 4
H = 4
FW = F * W
NEXT = 2 * W
TAP = 3 * CH
PACKED = 2048
F32 = jnp.float32
BF16 = jnp.bfloat16


def dot(a, b, contract):
    return lax.dot_general(a, b, (contract, ((), ())), preferred_element_type=F32)


def row_major():
    parts = []
    for h in range(H):
        pair = lax.broadcasted_iota(jnp.int32, (CH, H * CH), 1)
        channel = lax.broadcasted_iota(jnp.int32, (CH, H * CH), 0)
        parts.append(jnp.where(pair == channel * H + h, 1.0, 0.0).astype(BF16))
    return jnp.concatenate(parts, axis=0)


def frames(ref, count):
    return jnp.concatenate([ref[f] for f in range(count)], axis=1)


def shifted(value, step):
    lane = lax.broadcasted_iota(jnp.int32, (CH, W), 1)
    parts = []
    for f in range(value.shape[1] // W):
        part = pltpu.roll(value[:, f * W : (f + 1) * W], (-step) % W, 1)
        parts.append(jnp.where(lane == (W - 1 if step > 0 else 0), 0.0, part))
    return jnp.concatenate(parts, axis=1)


def column_taps(active):
    wide = active.astype(F32)
    return jnp.concatenate([shifted(wide, -1).astype(BF16), active, shifted(wide, 1).astype(BF16)], axis=0)


def rows_of(ref, first, count):
    return ref[first * CH : (first + count) * CH, :]


def normalize(x):
    scale = lax.rsqrt(jnp.sum(x * x, axis=0, keepdims=True) * (1.0 / CH) + 1e-06)
    return x * scale, scale


def sigmoid(x):
    return 1.0 / (1.0 + jnp.exp(-x))


def load_kernel(feat_in, cot_in, feat, cot, sems):
    copies = [
        pltpu.make_async_copy(cot_in, cot, sems.at[0]),
        pltpu.make_async_copy(feat_in, feat, sems.at[1]),
    ]
    for copy in copies:
        copy.start()
    for copy in copies:
        copy.wait()


def cot_kernel(cot, own, bottom, top):
    rows = dot(row_major(), frames(cot, F), ((1,), (0,))).astype(BF16)
    own[...] = rows
    top[...] = rows[:CH]
    bottom[...] = rows[(H - 1) * CH :]


def active_kernel(feat, act, normed, scale):
    values = dot(row_major(), frames(feat, F), ((1,), (0,)))
    for h in range(H):
        n, scale[h] = normalize(values[h * CH : (h + 1) * CH])
        normed[h] = n
        act[h] = column_taps((n * sigmoid(n)).astype(BF16))


def inner_kernel(own, act, wsum):
    def terms(first, count, h):
        rows = rows_of(own, first, count)
        return [dot(rows[:, (2 - t) * W :], act[h, :, : (t + 2) * W], ((1,), (1,))) for t in range(3)]

    second, third = terms(0, 3, 1), terms(1, 3, 2)
    first, last = terms(0, 2, 0), terms(2, 2, 3)
    for t in range(3):
        both = second[t] + third[t]
        wsum[t, :CH] = both[:CH] + last[t][:CH]
        wsum[t, CH : 2 * CH] = both[CH : 2 * CH] + first[t][:CH] + last[t][CH:]
        wsum[t, 2 * CH :] = both[2 * CH :] + first[t][CH:]


def past_kernel(before, own, inner_sum, wsum, past_act):
    values = dot(row_major(), frames(before, 2), ((1,), (0,)))
    sums = [inner_sum[t] for t in range(2)]
    zeros = jnp.zeros((CH, TAP), F32)
    for h in range(H):
        n, _ = normalize(values[h * CH : (h + 1) * CH])
        past = column_taps((n * sigmoid(n)).astype(BF16))
        if h in (0, H - 1):
            past_act[h // (H - 1)] = past
        rows = rows_of(own, max(h - 1, 0), 3 - (h in (0, H - 1)))
        for t in range(2):
            term = dot(rows[:, : (2 - t) * W], past[:, t * W :], ((1,), (1,)))
            term = jnp.concatenate([zeros] * (h == 0) + [term] + [zeros] * (h == H - 1), axis=0)
            sums[t] = sums[t] + term
    for t in range(2):
        wsum[t] = sums[t]
    wsum[2] = inner_sum[2]


def edge_kernel(above, below, own, act, past_act, wsum, packed, first_frames):
    upper, lower = above[...], below[...]
    first = jnp.concatenate([past_act[0], act[0]], axis=1)
    last = jnp.concatenate([past_act[1], act[H - 1]], axis=1)
    sums = []
    for t in range(3):
        from_above = dot(upper, first[:, t * W : t * W + FW], ((1,), (1,)))
        from_below = dot(lower, last[:, t * W : t * W + FW], ((1,), (1,)))
        sums.append(
            jnp.concatenate([wsum[t, :CH] + from_above, wsum[t, CH : 2 * CH], wsum[t, 2 * CH :] + from_below], axis=0)
        )
    first_frames[:CH, :] = upper[:, :NEXT]
    first_frames[CH : 5 * CH, :] = own[:, :NEXT]
    first_frames[5 * CH :, :] = lower[:, :NEXT]
    for t in range(3):
        for j in range(2):
            packed[(2 * t + j) * TAP : (2 * t + j + 1) * TAP, :] = sums[t][:, j * W : (j + 1) * W].astype(BF16)
    rests = [total[:, 2 * W :] for total in sums] + [jnp.zeros((TAP, W - CH), F32)]
    packed[6 * TAP : 7 * TAP, :] = jnp.concatenate(rests, axis=1).astype(BF16)
    packed[7 * TAP :, :] = jnp.zeros((PACKED - 7 * TAP, W), BF16)


def input_kernel(above, below, own, later, normed, scale, weights, grad_out, done):
    stacked = [
        jnp.concatenate([weights[t * 9 + (2 - k) * 3 + c].astype(F32) for c in range(3)], axis=1)
        for t in range(3)
        for k in range(3)
    ]
    by_out = jnp.concatenate(stacked, axis=0).T.astype(BF16)
    rows = jnp.concatenate([above[...], own[...], below[...]], axis=0)
    results = []
    for h in range(H):
        mine, ahead = rows[h * CH : (h + 3) * CH], rows_of(later, h, 3)
        windows = [
            jnp.concatenate([mine[:, (2 - t) * W :], ahead[:, : (2 - t) * W]], axis=1) if t < 2 else mine
            for t in range(3)
        ]
        products = dot(by_out, jnp.concatenate(windows, axis=0), ((1,), (0,)))
        grad = products[CH : 2 * CH] + shifted(products[:CH], 1) + shifted(products[2 * CH :], -1)
        n = normed[h]
        sigma = sigmoid(n)
        grad = grad * sigma * (1.0 + n * (1.0 - sigma))
        inner = jnp.sum(grad * n, axis=0, keepdims=True) * (1.0 / CH)
        result = scale[h] * (grad - n * inner) + mine[CH : 2 * CH].astype(F32)
        results.append(result.astype(BF16))
    placed = dot(row_major().astype(F32).T.astype(BF16), jnp.concatenate(results, axis=0), ((1,), (0,)))
    for f in range(F):
        grad_out[f] = placed[:, f * W : (f + 1) * W].astype(BF16)
    done[...] = jnp.zeros(done.shape, F32)


def sum_kernel(parts, *refs):
    out = refs[-1]
    total = parts[0].astype(F32)
    for i in range(1, parts.shape[0]):
        total = total + parts[i].astype(F32)
    total = total.astype(BF16)
    for i in range(out.shape[0]):
        out[i] = total


def unpack_kernel(norm_factor, packed, out, held, sems):
    rests = packed[6 * TAP : 7 * TAP, :].astype(F32)
    width = TAP - 2 * W
    copies = []
    for t in range(3):
        tiles = [packed[(2 * t + j) * TAP : (2 * t + j + 1) * TAP, :].astype(F32) for j in range(2)]
        block = jnp.concatenate(tiles + [rests[:, t * width : (t + 1) * width]], axis=1) * norm_factor
        for c in range(3):
            column = block[:, c * CH : (c + 1) * CH]
            for k in range(3):
                held[t, (2 - k) * 3 + c] = column[k * CH : (k + 1) * CH]
        copies.append(pltpu.make_async_copy(held.at[t], out.at[pl.ds(t * 9, 9)], sems.at[t]))
        copies[-1].start()
    for copy in copies:
        copy.wait()


def call(kernel, name, outs, args, flops=0, after=(), out_hbm=False, scratch=()):
    vmem, anywhere = pl.BlockSpec(memory_space=pltpu.VMEM), pl.BlockSpec(memory_space=pl.ANY)
    return pl.pallas_call(
        kernel,
        out_shape=tuple(jax.ShapeDtypeStruct(shape, dtype) for shape, dtype in outs),
        in_specs=[vmem] * len(args) + [anywhere] * len(after),
        out_specs=(anywhere if out_hbm else vmem,) * len(outs),
        scratch_shapes=scratch,
        compiler_params=pltpu.CompilerParams(vmem_limit_bytes=16 << 20),
        cost_estimate=pl.CostEstimate(flops=flops, bytes_accessed=4 << 20, transcendentals=0),
        name=name,
    )(*args, *after)


def sum_to_slots(parts, count, name, after=()):
    return call(sum_kernel, name, [((count,) + parts.shape[1:], BF16)], (parts,), after=after)[0]


def local(features, weights, cotangent):
    tm, rows = lax.axis_size(TM), lax.axis_size(ROWS)
    plane, depth = lax.axis_size(PLANE), lax.axis_size("z_pair")
    cells = F * tm * H * rows * W
    features = features.reshape(F, CH * H, W)
    cotangent = cotangent.reshape(F, CH * H, W)

    forward, back = [(i, i + 1) for i in range(tm - 1)], [(i + 1, i) for i in range(tm - 1)]
    before = lax.ppermute(features[F - 2 :], TM, forward)
    features, cotangent = call(
        load_kernel,
        "load",
        [((F, CH * H, W), BF16), ((F, CH * H, W), BF16)],
        (),
        after=[pltpu.with_memory_space_constraint(value, pltpu.HBM) for value in (features, cotangent)],
        scratch=[pltpu.SemaphoreType.DMA((2,))],
    )
    own, bottom, top = call(
        cot_kernel,
        "cot_rows",
        [((H * CH, FW), BF16), ((CH, FW), BF16), ((CH, FW), BF16)],
        (cotangent,),
        1 << 30,
    )
    above = lax.ppermute(bottom, ROWS, [(i, i + 1) for i in range(rows - 1)])
    below = lax.ppermute(top, ROWS, [(i + 1, i) for i in range(rows - 1)])
    act, normed, scale = call(
        active_kernel,
        "active",
        [((H, TAP, FW), BF16), ((H, CH, FW), F32), ((H, 1, FW), F32)],
        (features,),
        1 << 31,
    )
    (wsum,) = call(inner_kernel, "own_cells", [((3, TAP, TAP), F32)], (own, act), 1 << 31)
    wsum, past_act = call(
        past_kernel,
        "frames_before",
        [((3, TAP, TAP), F32), ((2, TAP, NEXT), BF16)],
        (before, own, wsum),
        1 << 30,
    )
    packed, first_frames = call(
        edge_kernel,
        "edge_rows",
        [((PACKED, W), BF16), (((H + 2) * CH, NEXT), BF16)],
        (above, below, own, act, past_act, wsum),
        1 << 30,
    )
    later = lax.ppermute(first_frames, TM, back)
    input_grad, done = call(
        input_kernel,
        "input_grad",
        [((F, CH * H, W), BF16), ((8, W), F32)],
        (above, below, own, later, normed, scale, weights.reshape(27, CH, CH)),
        1 << 31,
    )

    part = PACKED // plane
    parts = lax.all_to_all(packed.reshape(plane, part, W), PLANE, 0, 0)
    slabs = sum_to_slots(parts, depth, "plane_sum", after=())
    slabs = lax.all_to_all(slabs, "z_pair", 0, 0)
    whole = sum_to_slots(slabs, plane, "depth_sum", after=(done,))
    whole = lax.all_to_all(whole, PLANE, 0, 0).reshape(PACKED, W)

    (weight_grad,) = call(
        lambda *refs: unpack_kernel(1.0 / float(cells) ** 0.5, *refs),
        "unpack",
        [((27, CH, CH), F32)],
        (whole,),
        out_hbm=True,
        scratch=[pltpu.VMEM((3, 9, CH, CH), F32), pltpu.SemaphoreType.DMA((3,))],
    )
    return (input_grad.reshape(F, CH, H, W), weight_grad.reshape(3, 3, 3, CH, CH))


def solution(mesh):
    fine = Mesh(
        mesh.devices.reshape(2, 4, 2, 2, 8, 2), ("y_hi", "x", "core", "y_lo", "z_pair", "z_in")
    )
    return jax.shard_map(
        local,
        mesh=fine,
        in_specs=(P(TM, None, ROWS, None), P(), P(TM, None, ROWS, None)),
        out_specs=(P(TM, None, ROWS, None), P()),
        check_vma=False,
    )
```

```python
import jax
import jax.numpy as jnp
from jax import lax
from jax.experimental import pallas as pl
from jax.experimental.pallas import tpu as pltpu
from jax.sharding import Mesh, PartitionSpec as P

TM = ("y_hi", "x", "core")
ROWS = ("y_lo", "z_pair", "z_in")
NEAR = ("y_hi", "x", "y_lo", "z_in")
PLANE = ("core",) + NEAR
CH = 96
W = 128
F = 4
H = 4
FW = F * W
NEXT = 2 * W
TAP = 3 * CH
HALF = CH // 2
TILE = 3 * HALF
PACKED = 1024
F32 = jnp.float32
BF16 = jnp.bfloat16


def dot(a, b, contract):
    return lax.dot_general(a, b, (contract, ((), ())), preferred_element_type=F32)


def row_major():
    parts = []
    for h in range(H):
        pair = lax.broadcasted_iota(jnp.int32, (CH, H * CH), 1)
        channel = lax.broadcasted_iota(jnp.int32, (CH, H * CH), 0)
        parts.append(jnp.where(pair == channel * H + h, 1.0, 0.0).astype(BF16))
    return jnp.concatenate(parts, axis=0)


def frames(ref, count):
    return jnp.concatenate([ref[f] for f in range(count)], axis=1)


def shifted(value, step):
    lane = lax.broadcasted_iota(jnp.int32, (CH, W), 1)
    parts = []
    for f in range(value.shape[1] // W):
        part = pltpu.roll(value[:, f * W : (f + 1) * W], (-step) % W, 1)
        parts.append(jnp.where(lane == (W - 1 if step > 0 else 0), 0.0, part))
    return jnp.concatenate(parts, axis=1)


def column_taps(active):
    wide = active.astype(F32)
    return jnp.concatenate([shifted(wide, -1).astype(BF16), active, shifted(wide, 1).astype(BF16)], axis=0)


def rows_of(ref, first, count):
    return ref[first * CH : (first + count) * CH, :]


def normalize(x):
    scale = lax.rsqrt(jnp.sum(x * x, axis=0, keepdims=True) * (1.0 / CH) + 1e-06)
    return x * scale, scale


def sigmoid(x):
    return 1.0 / (1.0 + jnp.exp(-x))


def load_kernel(feat_in, cot_in, last_frames, feat, cot, sems):
    copies = [
        pltpu.make_async_copy(feat_in.at[pl.ds(F - 2, 2)], last_frames, sems.at[0]),
        pltpu.make_async_copy(cot_in, cot, sems.at[1]),
        pltpu.make_async_copy(feat_in, feat, sems.at[2]),
    ]
    for copy in copies:
        copy.start()
    for copy in copies:
        copy.wait()


def cot_kernel(cot, own, bottom, top):
    rows = dot(row_major(), frames(cot, F), ((1,), (0,))).astype(BF16)
    own[...] = rows
    top[...] = rows[:CH]
    bottom[...] = rows[(H - 1) * CH :]


def active_kernel(feat, act, normed, scale):
    values = dot(row_major(), frames(feat, F), ((1,), (0,)))
    for h in range(H):
        n, scale[h] = normalize(values[h * CH : (h + 1) * CH])
        normed[h] = n
        act[h] = column_taps((n * sigmoid(n)).astype(BF16))


def inner_kernel(own, act, wsum):
    def terms(first, count, h):
        rows = rows_of(own, first, count)
        return [dot(rows[:, (2 - t) * W :], act[h, :, : (t + 2) * W], ((1,), (1,))) for t in range(3)]

    second, third = terms(0, 3, 1), terms(1, 3, 2)
    first, last = terms(0, 2, 0), terms(2, 2, 3)
    for t in range(3):
        both = second[t] + third[t]
        wsum[t, :CH] = both[:CH] + last[t][:CH]
        wsum[t, CH : 2 * CH] = both[CH : 2 * CH] + first[t][:CH] + last[t][CH:]
        wsum[t, 2 * CH :] = both[2 * CH :] + first[t][CH:]


def past_kernel(before, own, inner_sum, wsum, past_act):
    values = dot(row_major(), frames(before, 2), ((1,), (0,)))
    sums = [inner_sum[t] for t in range(2)]
    zeros = jnp.zeros((CH, TAP), F32)
    for h in range(H):
        n, _ = normalize(values[h * CH : (h + 1) * CH])
        past = column_taps((n * sigmoid(n)).astype(BF16))
        if h in (0, H - 1):
            past_act[h // (H - 1)] = past
        rows = rows_of(own, max(h - 1, 0), 3 - (h in (0, H - 1)))
        for t in range(2):
            term = dot(rows[:, : (2 - t) * W], past[:, t * W :], ((1,), (1,)))
            term = jnp.concatenate([zeros] * (h == 0) + [term] + [zeros] * (h == H - 1), axis=0)
            sums[t] = sums[t] + term
    for t in range(2):
        wsum[t] = sums[t]
    wsum[2] = inner_sum[2]


def edge_kernel(above, below, own, act, past_act, wsum, packed, first_frames):
    upper, lower = above[...], below[...]
    first = jnp.concatenate([past_act[0], act[0]], axis=1)
    last = jnp.concatenate([past_act[1], act[H - 1]], axis=1)
    sums = []
    for t in range(3):
        from_above = dot(upper, first[:, t * W : t * W + FW], ((1,), (1,)))
        from_below = dot(lower, last[:, t * W : t * W + FW], ((1,), (1,)))
        sums.append(
            jnp.concatenate([wsum[t, :CH] + from_above, wsum[t, CH : 2 * CH], wsum[t, 2 * CH :] + from_below], axis=0)
        )
    first_frames[:CH, :] = upper[:, :NEXT]
    first_frames[CH : 5 * CH, :] = own[:, :NEXT]
    first_frames[5 * CH :, :] = lower[:, :NEXT]
    for half in range(2):
        picked = [
            jnp.concatenate([total[k * CH + half * HALF : k * CH + (half + 1) * HALF] for k in range(3)], axis=0)
            for total in sums
        ]
        for t in range(3):
            for j in range(2):
                packed[half, (2 * t + j) * TILE : (2 * t + j + 1) * TILE, :] = picked[t][:, j * W : (j + 1) * W].astype(BF16)
        rests = [total[:, 2 * W :] for total in picked] + [jnp.zeros((TILE, W - CH), F32)]
        packed[half, 6 * TILE : 7 * TILE, :] = jnp.concatenate(rests, axis=1).astype(BF16)
        packed[half, 7 * TILE :, :] = jnp.zeros((PACKED - 7 * TILE, W), BF16)


def input_kernel(above, below, own, later, normed, scale, weights, grad_out, done):
    stacked = [
        jnp.concatenate([weights[t * 9 + (2 - k) * 3 + c].astype(F32) for c in range(3)], axis=1)
        for t in range(3)
        for k in range(3)
    ]
    by_out = jnp.concatenate(stacked, axis=0).T.astype(BF16)
    rows = jnp.concatenate([above[...], own[...], below[...]], axis=0)
    results = []
    for h in range(H):
        mine, ahead = rows[h * CH : (h + 3) * CH], rows_of(later, h, 3)
        windows = [
            jnp.concatenate([mine[:, (2 - t) * W :], ahead[:, : (2 - t) * W]], axis=1) if t < 2 else mine
            for t in range(3)
        ]
        products = dot(by_out, jnp.concatenate(windows, axis=0), ((1,), (0,)))
        grad = products[CH : 2 * CH] + shifted(products[:CH], 1) + shifted(products[2 * CH :], -1)
        n = normed[h]
        sigma = sigmoid(n)
        grad = grad * sigma * (1.0 + n * (1.0 - sigma))
        inner = jnp.sum(grad * n, axis=0, keepdims=True) * (1.0 / CH)
        result = scale[h] * (grad - n * inner) + mine[CH : 2 * CH].astype(F32)
        results.append(result.astype(BF16))
    placed = dot(row_major().astype(F32).T.astype(BF16), jnp.concatenate(results, axis=0), ((1,), (0,)))
    for f in range(F):
        grad_out[f] = placed[:, f * W : (f + 1) * W].astype(BF16)
    done[...] = jnp.zeros(done.shape, F32)


def sum_kernel(parts, *refs):
    out = refs[-1]
    total = parts[0].astype(F32)
    for i in range(1, parts.shape[0]):
        total = total + parts[i].astype(F32)
    total = total.astype(BF16)
    for i in range(out.shape[0]):
        out[i] = total


def unpack_kernel(norm_factor, half, packed, *refs):
    out, held, sems = refs[-3:]
    rests = packed[6 * TILE : 7 * TILE, :].astype(F32)
    width = TAP - 2 * W
    place = pl.multiple_of(half[0] * HALF, HALF)
    copies = []
    for t in range(3):
        tiles = [packed[(2 * t + j) * TILE : (2 * t + j + 1) * TILE, :].astype(F32) for j in range(2)]
        block = jnp.concatenate(tiles + [rests[:, t * width : (t + 1) * width]], axis=1) * norm_factor
        for c in range(3):
            column = block[:, c * CH : (c + 1) * CH]
            for k in range(3):
                held[t, (2 - k) * 3 + c] = column[k * HALF : (k + 1) * HALF]
        copies.append(pltpu.make_async_copy(held.at[t], out.at[pl.ds(t * 9, 9), pl.ds(place, HALF)], sems.at[t]))
        copies[-1].start()
    for copy in copies:
        copy.wait()


def call(kernel, name, outs, args, flops=0, smem=(), after=(), out_hbm=False, scratch=(), aliases={}):
    vmem, anywhere = pl.BlockSpec(memory_space=pltpu.VMEM), pl.BlockSpec(memory_space=pl.ANY)
    return pl.pallas_call(
        kernel,
        out_shape=tuple(jax.ShapeDtypeStruct(shape, dtype) for shape, dtype in outs),
        in_specs=[pl.BlockSpec(memory_space=pltpu.SMEM)] * len(smem) + [vmem] * len(args) + [anywhere] * len(after),
        out_specs=(anywhere if out_hbm else vmem,) * len(outs),
        scratch_shapes=scratch,
        input_output_aliases=aliases,
        compiler_params=pltpu.CompilerParams(vmem_limit_bytes=16 << 20),
        cost_estimate=pl.CostEstimate(flops=flops, bytes_accessed=0, transcendentals=0),
        name=name,
    )(*smem, *args, *after)


def sum_to_slots(parts, count, name, after=()):
    return call(sum_kernel, name, [((count,) + parts.shape[1:], BF16)], (parts,), after=after)[0]


def local(features, weights, cotangent):
    tm, rows = lax.axis_size(TM), lax.axis_size(ROWS)
    plane, depth = lax.axis_size(PLANE), lax.axis_size("z_pair")
    cells = F * tm * H * rows * W
    features = features.reshape(F, CH * H, W)
    cotangent = cotangent.reshape(F, CH * H, W)

    forward, back = [(i, i + 1) for i in range(tm - 1)], [(i + 1, i) for i in range(tm - 1)]
    last_frames, features, cotangent = call(
        load_kernel,
        "load",
        [((2, CH * H, W), BF16), ((F, CH * H, W), BF16), ((F, CH * H, W), BF16)],
        (),
        after=[pltpu.with_memory_space_constraint(value, pltpu.HBM) for value in (features, cotangent)],
        scratch=[pltpu.SemaphoreType.DMA((3,))],
    )
    before = lax.ppermute(last_frames, TM, forward)
    own, bottom, top = call(
        cot_kernel,
        "cot_rows",
        [((H * CH, FW), BF16), ((CH, FW), BF16), ((CH, FW), BF16)],
        (cotangent,),
        1 << 33,
    )
    above = lax.ppermute(bottom, ROWS, [(i, i + 1) for i in range(rows - 1)])
    below = lax.ppermute(top, ROWS, [(i + 1, i) for i in range(rows - 1)])
    act, normed, scale = call(
        active_kernel,
        "active",
        [((H, TAP, FW), BF16), ((H, CH, FW), F32), ((H, 1, FW), F32)],
        (features,),
    )
    (wsum,) = call(inner_kernel, "own_cells", [((3, TAP, TAP), F32)], (own, act))
    wsum, past_act = call(
        past_kernel,
        "frames_before",
        [((3, TAP, TAP), F32), ((2, TAP, NEXT), BF16)],
        (before, own, wsum),
    )
    packed, first_frames = call(
        edge_kernel,
        "edge_rows",
        [((2, PACKED, W), BF16), (((H + 2) * CH, NEXT), BF16)],
        (above, below, own, act, past_act, wsum),
        1 << 30,
    )
    later = lax.ppermute(first_frames, TM, back)
    input_grad, done = call(
        input_kernel,
        "input_grad",
        [((F, CH * H, W), BF16), ((8, W), F32)],
        (above, below, own, later, normed, scale, weights.reshape(27, CH, CH)),
        1 << 31,
    )

    part = 2 * PACKED // plane
    parts = lax.all_to_all(packed.reshape(plane, part, W), PLANE, 0, 0)
    slabs = sum_to_slots(parts, depth, "plane_sum")
    slabs = lax.all_to_all(slabs, "z_pair", 0, 0)
    slots = sum_to_slots(slabs, plane // 2, "depth_sum", after=(done,))
    own_half = lax.all_to_all(slots, NEAR, 0, 0).reshape(PACKED, W)
    other_half = lax.ppermute(own_half, "core", [(0, 1), (1, 0)])

    core = lax.axis_index("core").astype(jnp.int32).reshape(1)
    weight_grad = ()
    for half, values in ((core, own_half), (1 - core, other_half)):
        weight_grad = call(
            lambda *refs: unpack_kernel(1.0 / float(cells) ** 0.5, *refs),
            "unpack",
            [((27, CH, CH), F32)],
            (values,),
            smem=(half,),
            after=weight_grad,
            out_hbm=True,
            scratch=[pltpu.VMEM((3, 9, HALF, CH), F32), pltpu.SemaphoreType.DMA((3,))],
            aliases={2: 0} if weight_grad else {},
        )
    return (input_grad.reshape(F, CH, H, W), weight_grad[0].reshape(3, 3, 3, CH, CH))


def solution(mesh):
    fine = Mesh(
        mesh.devices.reshape(2, 4, 2, 2, 8, 2), ("y_hi", "x", "core", "y_lo", "z_pair", "z_in")
    )
    return jax.shard_map(
        local,
        mesh=fine,
        in_specs=(P(TM, None, ROWS, None), P(), P(TM, None, ROWS, None)),
        out_specs=(P(TM, None, ROWS, None), P()),
        check_vma=False,
    )
```

```python
import jax
import jax.numpy as jnp
from jax import lax
from jax.experimental import pallas as pl
from jax.experimental.pallas import tpu as pltpu
from jax.sharding import Mesh, PartitionSpec as P

TM = ("y_hi", "x", "core")
ROWS = ("y_lo", "z_pair", "z_in")
NEAR = ("y_hi", "x", "y_lo", "z_in")
CH = 96
W = 128
F = 4
H = 4
FW = F * W
NEXT = 2 * W
TAP = 3 * CH
HALF = CH // 2
TILE = 3 * HALF
TILES = 7
PACKED = 1024
F32 = jnp.float32
BF16 = jnp.bfloat16


def dot(a, b, contract):
    return lax.dot_general(a, b, (contract, ((), ())), preferred_element_type=F32)


def row_major():
    parts = []
    for h in range(H):
        pair = lax.broadcasted_iota(jnp.int32, (CH, H * CH), 1)
        channel = lax.broadcasted_iota(jnp.int32, (CH, H * CH), 0)
        parts.append(jnp.where(pair == channel * H + h, 1.0, 0.0).astype(BF16))
    return jnp.concatenate(parts, axis=0)


def frames(ref, count):
    return jnp.concatenate([ref[f] for f in range(count)], axis=1)


def shifted(value, step):
    lane = lax.broadcasted_iota(jnp.int32, (CH, W), 1)
    parts = []
    for f in range(value.shape[1] // W):
        part = pltpu.roll(value[:, f * W : (f + 1) * W], (-step) % W, 1)
        parts.append(jnp.where(lane == (W - 1 if step > 0 else 0), 0.0, part))
    return jnp.concatenate(parts, axis=1)


def column_taps(active):
    wide = active.astype(F32)
    return jnp.concatenate([shifted(wide, -1).astype(BF16), active, shifted(wide, 1).astype(BF16)], axis=0)


def time_taps(past, active):
    return jnp.concatenate(
        [
            jnp.concatenate([past, active[:, : FW - NEXT]], axis=1),
            jnp.concatenate([past[:, W:], active[:, : FW - W]], axis=1),
            active,
        ],
        axis=0,
    )


def rows_of(ref, first, count):
    return ref[first * CH : (first + count) * CH, :]


def normalize(x):
    scale = lax.rsqrt(jnp.sum(x * x, axis=0, keepdims=True) * (1.0 / CH) + 1e-06)
    return x * scale, scale


def sigmoid(x):
    return 1.0 / (1.0 + jnp.exp(-x))


def load_kernel(feat_in, cot_in, last_frames, feat, cot, sems):
    copies = [
        pltpu.make_async_copy(feat_in.at[pl.ds(F - 2, 2)], last_frames, sems.at[0]),
        pltpu.make_async_copy(cot_in, cot, sems.at[1]),
        pltpu.make_async_copy(feat_in, feat, sems.at[2]),
    ]
    for copy in copies:
        copy.start()
    for copy in copies:
        copy.wait()


def cot_kernel(cot, own, bottom, top, order):
    order[...] = row_major()
    rows = dot(order[...], frames(cot, F), ((1,), (0,))).astype(BF16)
    own[...] = rows
    top[...] = rows[:CH]
    bottom[...] = rows[(H - 1) * CH :]


def active_kernel(feat, order, act, normed, scale):
    values = dot(order[...], frames(feat, F), ((1,), (0,)))
    for h in range(H):
        n, scale[h] = normalize(values[h * CH : (h + 1) * CH])
        normed[h] = n
        act[h] = column_taps((n * sigmoid(n)).astype(BF16))


def inner_kernel(own, act, wsum):
    def term(first, count, h):
        past = jnp.zeros((TAP, NEXT), BF16)
        return dot(rows_of(own, first, count), time_taps(past, act[h]), ((1,), (1,)))

    both = term(0, 3, 1) + term(1, 3, 2)
    first, last = term(0, 2, 0), term(2, 2, 3)
    wsum[:CH, :] = both[:CH] + last[:CH]
    wsum[CH : 2 * CH, :] = both[CH : 2 * CH] + first[:CH] + last[CH:]
    wsum[2 * CH :, :] = both[2 * CH :] + first[CH:]


def past_kernel(before, own, order, inner_sum, wsum, past_act):
    values = dot(order[...], frames(before, 2), ((1,), (0,)))
    zeros = jnp.zeros((CH, 2 * TAP), F32)
    early = jnp.zeros((TAP, 2 * TAP), F32)
    for h in range(H):
        n, _ = normalize(values[h * CH : (h + 1) * CH])
        past = column_taps((n * sigmoid(n)).astype(BF16))
        if h in (0, H - 1):
            past_act[h // (H - 1)] = past
        late = jnp.concatenate([past[:, W:], jnp.zeros((TAP, W), BF16)], axis=1)
        rows = rows_of(own, max(h - 1, 0), 3 - (h in (0, H - 1)))
        term = dot(rows[:, :NEXT], jnp.concatenate([past, late], axis=0), ((1,), (1,)))
        early = early + jnp.concatenate([zeros] * (h == 0) + [term] + [zeros] * (h == H - 1), axis=0)
    wsum[...] = inner_sum[...] + jnp.concatenate([early, jnp.zeros((TAP, TAP), F32)], axis=1)


def edge_kernel(core, above, below, own, act, past_act, wsum, kept, given, first_frames, total):
    upper, lower = above[...], below[...]
    from_above = dot(upper, time_taps(past_act[0], act[0]), ((1,), (1,)))
    from_below = dot(lower, time_taps(past_act[1], act[H - 1]), ((1,), (1,)))
    first_frames[:CH, :] = upper[:, :NEXT]
    first_frames[CH : 5 * CH, :] = own[:, :NEXT]
    first_frames[5 * CH :, :] = lower[:, :NEXT]
    total[:CH, : 3 * TAP] = wsum[:CH] + from_above
    total[CH : 2 * CH, : 3 * TAP] = wsum[CH : 2 * CH]
    total[2 * CH :, : 3 * TAP] = wsum[2 * CH :] + from_below
    total[:, 3 * TAP :] = jnp.zeros((TAP, TILES * W - 3 * TAP), F32)
    for out, half in ((given, 1 - core[0]), (kept, core[0])):
        for k in range(3):
            rows = pl.ds(pl.multiple_of(k * CH + half * HALF, HALF), HALF)
            for j in range(TILES):
                tile = total[rows, j * W : (j + 1) * W]
                out[j * TILE + k * HALF : j * TILE + (k + 1) * HALF, :] = tile.astype(out.dtype)
        out[TILES * TILE :, :] = jnp.zeros((PACKED - TILES * TILE, W), out.dtype)


def add_kernel(kept, received, out):
    out[...] = (kept[...] + received[...].astype(F32)).astype(BF16)


def input_kernel(above, below, own, later, normed, scale, weights, grad_out, done):
    stacked = [
        jnp.concatenate([weights[t * 9 + (2 - k) * 3 + c].astype(F32) for c in range(3)], axis=1)
        for t in range(3)
        for k in range(3)
    ]
    by_out = jnp.concatenate(stacked, axis=0).T.astype(BF16)
    rows = jnp.concatenate([above[...], own[...], below[...]], axis=0)
    results = []
    for h in range(H):
        mine, ahead = rows[h * CH : (h + 3) * CH], rows_of(later, h, 3)
        windows = [
            jnp.concatenate([mine[:, (2 - t) * W :], ahead[:, : (2 - t) * W]], axis=1) if t < 2 else mine
            for t in range(3)
        ]
        products = dot(by_out, jnp.concatenate(windows, axis=0), ((1,), (0,)))
        grad = products[CH : 2 * CH] + shifted(products[:CH], 1) + shifted(products[2 * CH :], -1)
        n = normed[h]
        sigma = sigmoid(n)
        grad = grad * sigma * (1.0 + n * (1.0 - sigma))
        inner = jnp.sum(grad * n, axis=0, keepdims=True) * (1.0 / CH)
        result = scale[h] * (grad - n * inner) + mine[CH : 2 * CH].astype(F32)
        results.append(result.astype(BF16))
    placed = dot(row_major().astype(F32).T.astype(BF16), jnp.concatenate(results, axis=0), ((1,), (0,)))
    for f in range(F):
        grad_out[f] = placed[:, f * W : (f + 1) * W].astype(BF16)
    done[...] = jnp.zeros(done.shape, F32)


def sum_kernel(parts, *refs):
    out = refs[-1]
    total = parts[0].astype(F32)
    for i in range(1, parts.shape[0]):
        total = total + parts[i].astype(F32)
    total = total.astype(BF16)
    for i in range(out.shape[0]):
        out[i] = total


def unpack_kernel(norm_factor, half, packed, *refs):
    out, held, sems = refs[-3:]
    place = pl.multiple_of(half[0] * HALF, HALF)
    block = jnp.concatenate([packed[j * TILE : (j + 1) * TILE, :].astype(F32) for j in range(TILES)], axis=1) * norm_factor
    copies = []
    for t in range(3):
        for c in range(3):
            column = block[:, (t * 3 + c) * CH : (t * 3 + c + 1) * CH]
            for k in range(3):
                held[t, (2 - k) * 3 + c] = column[k * HALF : (k + 1) * HALF]
        copies.append(pltpu.make_async_copy(held.at[t], out.at[pl.ds(t * 9, 9), pl.ds(place, HALF)], sems.at[t]))
        copies[-1].start()
    for copy in copies:
        copy.wait()


def call(kernel, name, outs, args, flops=0, smem=(), after=(), out_hbm=(), scratch=(), aliases={}):
    vmem, anywhere = pl.BlockSpec(memory_space=pltpu.VMEM), pl.BlockSpec(memory_space=pl.ANY)
    return pl.pallas_call(
        kernel,
        out_shape=tuple(jax.ShapeDtypeStruct(shape, dtype) for shape, dtype in outs),
        in_specs=[pl.BlockSpec(memory_space=pltpu.SMEM)] * len(smem) + [vmem] * len(args) + [anywhere] * len(after),
        out_specs=tuple(anywhere if i in out_hbm else vmem for i in range(len(outs))),
        scratch_shapes=scratch,
        input_output_aliases=aliases,
        compiler_params=pltpu.CompilerParams(vmem_limit_bytes=16 << 20),
        cost_estimate=pl.CostEstimate(flops=flops, bytes_accessed=0, transcendentals=0),
        name=name,
    )(*smem, *args, *after)


def sum_to_slots(parts, count, name, after=()):
    return call(sum_kernel, name, [((count,) + parts.shape[1:], BF16)], (parts,), after=after)[0]


def local(features, weights, cotangent):
    tm, rows = lax.axis_size(TM), lax.axis_size(ROWS)
    near, depth = lax.axis_size(NEAR), lax.axis_size("z_pair")
    cells = F * tm * H * rows * W
    features = features.reshape(F, CH * H, W)
    cotangent = cotangent.reshape(F, CH * H, W)

    forward, back = [(i, i + 1) for i in range(tm - 1)], [(i + 1, i) for i in range(tm - 1)]
    last_frames, features, cotangent = call(
        load_kernel,
        "load",
        [((2, CH * H, W), BF16), ((F, CH * H, W), BF16), ((F, CH * H, W), BF16)],
        (),
        after=[pltpu.with_memory_space_constraint(value, pltpu.HBM) for value in (features, cotangent)],
        scratch=[pltpu.SemaphoreType.DMA((3,))],
    )
    before = lax.ppermute(last_frames, TM, forward)
    own, bottom, top, order = call(
        cot_kernel,
        "cot_rows",
        [((H * CH, FW), BF16), ((CH, FW), BF16), ((CH, FW), BF16), ((H * CH, H * CH), BF16)],
        (cotangent,),
        1 << 33,
    )
    above = lax.ppermute(bottom, ROWS, [(i, i + 1) for i in range(rows - 1)])
    below = lax.ppermute(top, ROWS, [(i + 1, i) for i in range(rows - 1)])
    act, normed, scale = call(
        active_kernel,
        "active",
        [((H, TAP, FW), BF16), ((H, CH, FW), F32), ((H, 1, FW), F32)],
        (features, order),
    )
    (wsum,) = call(inner_kernel, "own_cells", [((TAP, 3 * TAP), F32)], (own, act))
    wsum, past_act = call(
        past_kernel,
        "frames_before",
        [((TAP, 3 * TAP), F32), ((2, TAP, NEXT), BF16)],
        (before, own, order, wsum),
    )
    core = lax.axis_index("core").astype(jnp.int32).reshape(1)
    kept, given, first_frames = call(
        edge_kernel,
        "edge_rows",
        [((PACKED, W), F32), ((PACKED, W), BF16), (((H + 2) * CH, NEXT), BF16)],
        (above, below, own, act, past_act, wsum),
        smem=(core,),
        scratch=[pltpu.VMEM((TAP, TILES * W), F32)],
    )
    received = lax.ppermute(given, "core", [(0, 1), (1, 0)])
    later = lax.ppermute(first_frames, TM, back)
    input_grad, done = call(
        input_kernel,
        "input_grad",
        [((F, CH * H, W), BF16), ((8, W), F32)],
        (above, below, own, later, normed, scale, weights.reshape(27, CH, CH)),
        1 << 31,
    )

    (packed,) = call(add_kernel, "core_sum", [((PACKED, W), BF16)], (kept, received))
    parts = lax.all_to_all(packed.reshape(near, PACKED // near, W), NEAR, 0, 0)
    slabs = sum_to_slots(parts, depth, "plane_sum")
    slabs = lax.all_to_all(slabs, "z_pair", 0, 0)
    slots = sum_to_slots(slabs, near, "depth_sum", after=(done,))
    own_half = lax.all_to_all(slots, NEAR, 0, 0).reshape(PACKED, W)
    other_half = lax.ppermute(own_half, "core", [(0, 1), (1, 0)])

    weight_grad = ()
    for half, values in ((core, own_half), (1 - core, other_half)):
        weight_grad = call(
            lambda *refs: unpack_kernel(1.0 / float(cells) ** 0.5, *refs),
            "unpack",
            [((27, CH, CH), F32)],
            (values,),
            smem=(half,),
            after=weight_grad,
            out_hbm=(0,),
            scratch=[pltpu.VMEM((3, 9, HALF, CH), F32), pltpu.SemaphoreType.DMA((3,))],
            aliases={2: 0} if weight_grad else {},
        )
    return (input_grad.reshape(F, CH, H, W), weight_grad[0].reshape(3, 3, 3, CH, CH))


def solution(mesh):
    fine = Mesh(
        mesh.devices.reshape(2, 4, 2, 2, 8, 2), ("y_hi", "x", "core", "y_lo", "z_pair", "z_in")
    )
    return jax.shard_map(
        local,
        mesh=fine,
        in_specs=(P(TM, None, ROWS, None), P(), P(TM, None, ROWS, None)),
        out_specs=(P(TM, None, ROWS, None), P()),
        check_vma=False,
    )
```

```python
import jax
import jax.numpy as jnp
from jax import lax
from jax.experimental import pallas as pl
from jax.experimental.pallas import tpu as pltpu
from jax.sharding import Mesh, PartitionSpec as P

TM = ("y_hi", "x", "core")
ROWS = ("y_lo", "z_pair", "z_in")
NEAR = ("y_hi", "x", "y_lo", "z_in")
CH = 96
W = 128
F = 4
H = 4
FW = F * W
NEXT = 2 * W
TAP = 3 * CH
HALF = CH // 2
TILE = 3 * HALF
TILES = 7
PACKED = 1024
F32 = jnp.float32
BF16 = jnp.bfloat16


def dot(a, b, contract):
    return lax.dot_general(a, b, (contract, ((), ())), preferred_element_type=F32)


def row_major():
    parts = []
    for h in range(H):
        pair = lax.broadcasted_iota(jnp.int32, (CH, H * CH), 1)
        channel = lax.broadcasted_iota(jnp.int32, (CH, H * CH), 0)
        parts.append(jnp.where(pair == channel * H + h, 1.0, 0.0).astype(BF16))
    return jnp.concatenate(parts, axis=0)


def frames(ref, count):
    return jnp.concatenate([ref[f] for f in range(count)], axis=1)


def shifted(value, step):
    lane = lax.broadcasted_iota(jnp.int32, (CH, W), 1)
    parts = []
    for f in range(value.shape[1] // W):
        part = pltpu.roll(value[:, f * W : (f + 1) * W], (-step) % W, 1)
        parts.append(jnp.where(lane == (W - 1 if step > 0 else 0), 0.0, part))
    return jnp.concatenate(parts, axis=1)


def column_taps(active):
    wide = active.astype(F32)
    return jnp.concatenate([shifted(wide, -1).astype(BF16), active, shifted(wide, 1).astype(BF16)], axis=0)


def time_taps(past, active):
    return jnp.concatenate(
        [
            jnp.concatenate([past, active[:, : FW - NEXT]], axis=1),
            jnp.concatenate([past[:, W:], active[:, : FW - W]], axis=1),
            active,
        ],
        axis=0,
    )


def rows_of(ref, first, count):
    return ref[first * CH : (first + count) * CH, :]


def normalize(x):
    scale = lax.rsqrt(jnp.sum(x * x, axis=0, keepdims=True) * (1.0 / CH) + 1e-06)
    return x * scale, scale


def sigmoid(x):
    return 1.0 / (1.0 + jnp.exp(-x))


def load_kernel(feat_in, cot_in, last_frames, feat, cot, sems):
    copies = [
        pltpu.make_async_copy(feat_in.at[pl.ds(F - 2, 2)], last_frames, sems.at[0]),
        pltpu.make_async_copy(cot_in, cot, sems.at[1]),
        pltpu.make_async_copy(feat_in, feat, sems.at[2]),
    ]
    for copy in copies:
        copy.start()
    for copy in copies:
        copy.wait()


def cot_kernel(cot, own, bottom, top, order):
    order[...] = row_major()
    rows = dot(order[...], frames(cot, F), ((1,), (0,))).astype(BF16)
    own[...] = rows
    top[...] = rows[:CH]
    bottom[...] = rows[(H - 1) * CH :]


def active_kernel(feat, order, act, normed, scale):
    values = dot(order[...], frames(feat, F), ((1,), (0,)))
    for h in range(H):
        n, scale[h] = normalize(values[h * CH : (h + 1) * CH])
        normed[h] = n
        act[h] = column_taps((n * sigmoid(n)).astype(BF16))


def inner_kernel(own, act, wsum):
    def term(first, count, h):
        past = jnp.zeros((TAP, NEXT), BF16)
        return dot(rows_of(own, first, count), time_taps(past, act[h]), ((1,), (1,)))

    both = term(0, 3, 1) + term(1, 3, 2)
    first, last = term(0, 2, 0), term(2, 2, 3)
    wsum[:CH, :] = both[:CH] + last[:CH]
    wsum[CH : 2 * CH, :] = both[CH : 2 * CH] + first[:CH] + last[CH:]
    wsum[2 * CH :, :] = both[2 * CH :] + first[CH:]


def past_kernel(before, own, order, inner_sum, wsum, past_act):
    values = dot(order[...], frames(before, 2), ((1,), (0,)))
    zeros = jnp.zeros((CH, 2 * TAP), F32)
    early = jnp.zeros((TAP, 2 * TAP), F32)
    for h in range(H):
        n, _ = normalize(values[h * CH : (h + 1) * CH])
        past = column_taps((n * sigmoid(n)).astype(BF16))
        if h in (0, H - 1):
            past_act[h // (H - 1)] = past
        late = jnp.concatenate([past[:, W:], jnp.zeros((TAP, W), BF16)], axis=1)
        rows = rows_of(own, max(h - 1, 0), 3 - (h in (0, H - 1)))
        term = dot(rows[:, :NEXT], jnp.concatenate([past, late], axis=0), ((1,), (1,)))
        early = early + jnp.concatenate([zeros] * (h == 0) + [term] + [zeros] * (h == H - 1), axis=0)
    wsum[...] = inner_sum[...] + jnp.concatenate([early, jnp.zeros((TAP, TAP), F32)], axis=1)


def edge_kernel(core, above, below, own, act, past_act, wsum, kept, given, first_frames, total):
    upper, lower = above[...], below[...]
    from_above = dot(upper, time_taps(past_act[0], act[0]), ((1,), (1,)))
    from_below = dot(lower, time_taps(past_act[1], act[H - 1]), ((1,), (1,)))
    first_frames[:CH, :] = upper[:, :NEXT]
    first_frames[CH : 5 * CH, :] = own[:, :NEXT]
    first_frames[5 * CH :, :] = lower[:, :NEXT]
    total[:CH, : 3 * TAP] = wsum[:CH] + from_above
    total[CH : 2 * CH, : 3 * TAP] = wsum[CH : 2 * CH]
    total[2 * CH :, : 3 * TAP] = wsum[2 * CH :] + from_below
    total[:, 3 * TAP :] = jnp.zeros((TAP, TILES * W - 3 * TAP), F32)
    for out, half in ((given, 1 - core[0]), (kept, core[0])):
        for k in range(3):
            rows = pl.ds(pl.multiple_of(k * CH + half * HALF, HALF), HALF)
            for j in range(TILES):
                tile = total[rows, j * W : (j + 1) * W]
                out[j * TILE + k * HALF : j * TILE + (k + 1) * HALF, :] = tile.astype(out.dtype)
        out[TILES * TILE :, :] = jnp.zeros((PACKED - TILES * TILE, W), out.dtype)


def add_kernel(core, kept, exchanged, out):
    out[...] = (kept[...] + exchanged[1 - core[0]].astype(F32)).astype(BF16)


def input_kernel(above, below, own, later, normed, scale, weights, grad_out, done):
    stacked = [
        jnp.concatenate([weights[t * 9 + (2 - k) * 3 + c].astype(F32) for c in range(3)], axis=1)
        for t in range(3)
        for k in range(3)
    ]
    by_out = jnp.concatenate(stacked, axis=0).T.astype(BF16)
    rows = jnp.concatenate([above[...], own[...], below[...]], axis=0)
    results = []
    for h in range(H):
        mine, ahead = rows[h * CH : (h + 3) * CH], rows_of(later, h, 3)
        windows = [
            jnp.concatenate([mine[:, (2 - t) * W :], ahead[:, : (2 - t) * W]], axis=1) if t < 2 else mine
            for t in range(3)
        ]
        products = dot(by_out, jnp.concatenate(windows, axis=0), ((1,), (0,)))
        grad = products[CH : 2 * CH] + shifted(products[:CH], 1) + shifted(products[2 * CH :], -1)
        n = normed[h]
        sigma = sigmoid(n)
        grad = grad * sigma * (1.0 + n * (1.0 - sigma))
        inner = jnp.sum(grad * n, axis=0, keepdims=True) * (1.0 / CH)
        result = scale[h] * (grad - n * inner) + mine[CH : 2 * CH].astype(F32)
        results.append(result.astype(BF16))
    placed = dot(row_major().astype(F32).T.astype(BF16), jnp.concatenate(results, axis=0), ((1,), (0,)))
    for f in range(F):
        grad_out[f] = placed[:, f * W : (f + 1) * W].astype(BF16)
    done[...] = jnp.zeros(done.shape, F32)


def sum_kernel(parts, *refs):
    out = refs[-1]
    total = parts[0].astype(F32)
    for i in range(1, parts.shape[0]):
        total = total + parts[i].astype(F32)
    total = total.astype(BF16)
    for i in range(out.shape[0]):
        out[i] = total


def unpack_kernel(norm_factor, packed, out, held, sems):
    copies = []
    blocks = [
        jnp.concatenate([packed[half, j * TILE : (j + 1) * TILE, :].astype(F32) for j in range(TILES)], axis=1)
        * norm_factor
        for half in range(2)
    ]
    for t in range(3):
        for c in range(3):
            for half in range(2):
                column = blocks[half][:, (t * 3 + c) * CH : (t * 3 + c + 1) * CH]
                for k in range(3):
                    held[t * 9 + (2 - k) * 3 + c, half * HALF : (half + 1) * HALF] = column[k * HALF : (k + 1) * HALF]
        copies.append(pltpu.make_async_copy(held.at[pl.ds(t * 9, 9)], out.at[pl.ds(t * 9, 9)], sems.at[t]))
        copies[-1].start()
    for copy in copies:
        copy.wait()


def call(kernel, name, outs, args, flops=0, smem=(), after=(), out_hbm=(), scratch=(), aliases={}):
    vmem, anywhere = pl.BlockSpec(memory_space=pltpu.VMEM), pl.BlockSpec(memory_space=pl.ANY)
    return pl.pallas_call(
        kernel,
        out_shape=tuple(jax.ShapeDtypeStruct(shape, dtype) for shape, dtype in outs),
        in_specs=[pl.BlockSpec(memory_space=pltpu.SMEM)] * len(smem) + [vmem] * len(args) + [anywhere] * len(after),
        out_specs=tuple(anywhere if i in out_hbm else vmem for i in range(len(outs))),
        scratch_shapes=scratch,
        input_output_aliases=aliases,
        compiler_params=pltpu.CompilerParams(vmem_limit_bytes=16 << 20),
        cost_estimate=pl.CostEstimate(flops=flops, bytes_accessed=0, transcendentals=0),
        name=name,
    )(*smem, *args, *after)


def sum_to_slots(parts, count, name, after=()):
    return call(sum_kernel, name, [((count,) + parts.shape[1:], BF16)], (parts,), after=after)[0]


def local(features, weights, cotangent):
    tm, rows = lax.axis_size(TM), lax.axis_size(ROWS)
    near, depth = lax.axis_size(NEAR), lax.axis_size("z_pair")
    cells = F * tm * H * rows * W
    features = features.reshape(F, CH * H, W)
    cotangent = cotangent.reshape(F, CH * H, W)

    forward, back = [(i, i + 1) for i in range(tm - 1)], [(i + 1, i) for i in range(tm - 1)]
    last_frames, features, cotangent = call(
        load_kernel,
        "load",
        [((2, CH * H, W), BF16), ((F, CH * H, W), BF16), ((F, CH * H, W), BF16)],
        (),
        after=[pltpu.with_memory_space_constraint(value, pltpu.HBM) for value in (features, cotangent)],
        scratch=[pltpu.SemaphoreType.DMA((3,))],
    )
    before = lax.ppermute(last_frames, TM, forward)
    own, bottom, top, order = call(
        cot_kernel,
        "cot_rows",
        [((H * CH, FW), BF16), ((CH, FW), BF16), ((CH, FW), BF16), ((H * CH, H * CH), BF16)],
        (cotangent,),
        1 << 33,
    )
    above = lax.ppermute(bottom, ROWS, [(i, i + 1) for i in range(rows - 1)])
    below = lax.ppermute(top, ROWS, [(i + 1, i) for i in range(rows - 1)])
    act, normed, scale = call(
        active_kernel,
        "active",
        [((H, TAP, FW), BF16), ((H, CH, FW), F32), ((H, 1, FW), F32)],
        (features, order),
    )
    (wsum,) = call(inner_kernel, "own_cells", [((TAP, 3 * TAP), F32)], (own, act))
    wsum, past_act = call(
        past_kernel,
        "frames_before",
        [((TAP, 3 * TAP), F32), ((2, TAP, NEXT), BF16)],
        (before, own, order, wsum),
    )
    core = lax.axis_index("core").astype(jnp.int32).reshape(1)
    kept, given, first_frames = call(
        edge_kernel,
        "edge_rows",
        [((PACKED, W), F32), ((PACKED, W), BF16), (((H + 2) * CH, NEXT), BF16)],
        (above, below, own, act, past_act, wsum),
        smem=(core,),
        scratch=[pltpu.VMEM((TAP, TILES * W), F32)],
    )
    exchanged = lax.all_gather(given, "core")
    later = lax.ppermute(first_frames, TM, back)
    input_grad, done = call(
        input_kernel,
        "input_grad",
        [((F, CH * H, W), BF16), ((8, W), F32)],
        (above, below, own, later, normed, scale, weights.reshape(27, CH, CH)),
        1 << 31,
    )

    (packed,) = call(add_kernel, "core_sum", [((PACKED, W), BF16)], (kept, exchanged), smem=(core,))
    parts = lax.all_to_all(packed.reshape(near, PACKED // near, W), NEAR, 0, 0)
    slabs = sum_to_slots(parts, depth, "plane_sum")
    slabs = lax.all_to_all(slabs, "z_pair", 0, 0)
    slots = sum_to_slots(slabs, near, "depth_sum", after=(done,))
    own_half = lax.all_to_all(slots, NEAR, 0, 0).reshape(PACKED, W)
    whole = lax.all_gather(own_half, "core")
    (weight_grad,) = call(
        lambda *refs: unpack_kernel(1.0 / float(cells) ** 0.5, *refs),
        "unpack",
        [((27, CH, CH), F32)],
        (whole,),
        out_hbm=(0,),
        scratch=[pltpu.VMEM((27, CH, CH), F32), pltpu.SemaphoreType.DMA((3,))],
    )
    return (input_grad.reshape(F, CH, H, W), weight_grad.reshape(3, 3, 3, CH, CH))


def solution(mesh):
    fine = Mesh(
        mesh.devices.reshape(2, 4, 2, 2, 8, 2), ("y_hi", "x", "core", "y_lo", "z_pair", "z_in")
    )
    return jax.shard_map(
        local,
        mesh=fine,
        in_specs=(P(TM, None, ROWS, None), P(), P(TM, None, ROWS, None)),
        out_specs=(P(TM, None, ROWS, None), P()),
        check_vma=False,
    )
```

```python
import jax
import jax.numpy as jnp
from jax import lax
from jax.experimental import pallas as pl
from jax.experimental.pallas import tpu as pltpu
from jax.sharding import Mesh, PartitionSpec as P

TM = ("y_hi", "x", "core")
ROWS = ("y_lo", "z_pair", "z_in")
NEAR = ("y_hi", "x", "y_lo", "z_in")
CH = 96
W = 128
F = 4
H = 4
FW = F * W
NEXT = 2 * W
TAP = 3 * CH
HALF = CH // 2
TILE = 3 * HALF
TILES = 7
PACKED = 1024
F32 = jnp.float32
BF16 = jnp.bfloat16


def dot(a, b, contract):
    return lax.dot_general(a, b, (contract, ((), ())), preferred_element_type=F32)


def row_major():
    parts = []
    for h in range(H):
        pair = lax.broadcasted_iota(jnp.int32, (CH, H * CH), 1)
        channel = lax.broadcasted_iota(jnp.int32, (CH, H * CH), 0)
        parts.append(jnp.where(pair == channel * H + h, 1.0, 0.0).astype(BF16))
    return jnp.concatenate(parts, axis=0)


def frames(ref, count):
    return jnp.concatenate([ref[f] for f in range(count)], axis=1)


def shifted(value, step):
    lane = lax.broadcasted_iota(jnp.int32, (CH, W), 1)
    parts = []
    for f in range(value.shape[1] // W):
        part = pltpu.roll(value[:, f * W : (f + 1) * W], (-step) % W, 1)
        parts.append(jnp.where(lane == (W - 1 if step > 0 else 0), 0.0, part))
    return jnp.concatenate(parts, axis=1)


def column_taps(active):
    wide = active.astype(F32)
    return jnp.concatenate([shifted(wide, -1).astype(BF16), active, shifted(wide, 1).astype(BF16)], axis=0)


def time_taps(past, active):
    return jnp.concatenate(
        [
            jnp.concatenate([past, active[:, : FW - NEXT]], axis=1),
            jnp.concatenate([past[:, W:], active[:, : FW - W]], axis=1),
            active,
        ],
        axis=0,
    )


def rows_of(ref, first, count):
    return ref[first * CH : (first + count) * CH, :]


def normalize(x):
    scale = lax.rsqrt(jnp.sum(x * x, axis=0, keepdims=True) * (1.0 / CH) + 1e-06)
    return x * scale, scale


def sigmoid(x):
    return 1.0 / (1.0 + jnp.exp(-x))


def load_kernel(feat_in, cot_in, last_frames, feat, cot, sems):
    copies = [
        pltpu.make_async_copy(feat_in.at[pl.ds(F - 2, 2)], last_frames, sems.at[0]),
        pltpu.make_async_copy(cot_in, cot, sems.at[1]),
        pltpu.make_async_copy(feat_in, feat, sems.at[2]),
    ]
    for copy in copies:
        copy.start()
    for copy in copies:
        copy.wait()


def cot_kernel(cot, own, bottom, top, order):
    order[...] = row_major()
    rows = dot(order[...], frames(cot, F), ((1,), (0,))).astype(BF16)
    own[...] = rows
    top[...] = rows[:CH]
    bottom[...] = rows[(H - 1) * CH :]


def active_kernel(feat, order, act, normed, scale):
    values = dot(order[...], frames(feat, F), ((1,), (0,)))
    for h in range(H):
        n, scale[h] = normalize(values[h * CH : (h + 1) * CH])
        normed[h] = n
        act[h] = column_taps((n * sigmoid(n)).astype(BF16))


def inner_kernel(own, act, wsum):
    def term(first, count, h):
        past = jnp.zeros((TAP, NEXT), BF16)
        return dot(rows_of(own, first, count), time_taps(past, act[h]), ((1,), (1,)))

    both = term(0, 3, 1) + term(1, 3, 2)
    first, last = term(0, 2, 0), term(2, 2, 3)
    wsum[:CH, :] = both[:CH] + last[:CH]
    wsum[CH : 2 * CH, :] = both[CH : 2 * CH] + first[:CH] + last[CH:]
    wsum[2 * CH :, :] = both[2 * CH :] + first[CH:]


def past_kernel(before, own, order, inner_sum, wsum, past_act):
    values = dot(order[...], frames(before, 2), ((1,), (0,)))
    zeros = jnp.zeros((CH, 2 * TAP), F32)
    early = jnp.zeros((TAP, 2 * TAP), F32)
    for h in range(H):
        n, _ = normalize(values[h * CH : (h + 1) * CH])
        past = column_taps((n * sigmoid(n)).astype(BF16))
        if h in (0, H - 1):
            past_act[h // (H - 1)] = past
        late = jnp.concatenate([past[:, W:], jnp.zeros((TAP, W), BF16)], axis=1)
        rows = rows_of(own, max(h - 1, 0), 3 - (h in (0, H - 1)))
        term = dot(rows[:, :NEXT], jnp.concatenate([past, late], axis=0), ((1,), (1,)))
        early = early + jnp.concatenate([zeros] * (h == 0) + [term] + [zeros] * (h == H - 1), axis=0)
    wsum[...] = inner_sum[...] + jnp.concatenate([early, jnp.zeros((TAP, TAP), F32)], axis=1)


def edge_kernel(core, above, below, own, act, past_act, wsum, kept, given, first_frames, total):
    upper, lower = above[...], below[...]
    from_above = dot(upper, time_taps(past_act[0], act[0]), ((1,), (1,)))
    from_below = dot(lower, time_taps(past_act[1], act[H - 1]), ((1,), (1,)))
    first_frames[:CH, :] = upper[:, :NEXT]
    first_frames[CH : 5 * CH, :] = own[:, :NEXT]
    first_frames[5 * CH :, :] = lower[:, :NEXT]
    total[:CH, : 3 * TAP] = wsum[:CH] + from_above
    total[CH : 2 * CH, : 3 * TAP] = wsum[CH : 2 * CH]
    total[2 * CH :, : 3 * TAP] = wsum[2 * CH :] + from_below
    total[:, 3 * TAP :] = jnp.zeros((TAP, TILES * W - 3 * TAP), F32)
    for out, half in ((given, 1 - core[0]), (kept, core[0])):
        for k in range(3):
            rows = pl.ds(pl.multiple_of(k * CH + half * HALF, HALF), HALF)
            for j in range(TILES):
                tile = total[rows, j * W : (j + 1) * W]
                out[j * TILE + k * HALF : j * TILE + (k + 1) * HALF, :] = tile.astype(out.dtype)
        out[TILES * TILE :, :] = jnp.zeros((PACKED - TILES * TILE, W), out.dtype)


def add_kernel(core, kept, exchanged, out):
    out[...] = (kept[...] + exchanged[1 - core[0]].astype(F32)).astype(BF16)


def input_kernel(above, below, own, later, normed, scale, weights, grad_out, done):
    stacked = [
        jnp.concatenate([weights[t * 9 + (2 - k) * 3 + c].astype(F32) for c in range(3)], axis=1)
        for t in range(3)
        for k in range(3)
    ]
    by_out = jnp.concatenate(stacked, axis=0).T.astype(BF16)
    rows = jnp.concatenate([above[...], own[...], below[...]], axis=0)
    results = []
    for h in range(H):
        mine, ahead = rows[h * CH : (h + 3) * CH], rows_of(later, h, 3)
        windows = [
            jnp.concatenate([mine[:, (2 - t) * W :], ahead[:, : (2 - t) * W]], axis=1) if t < 2 else mine
            for t in range(3)
        ]
        products = dot(by_out, jnp.concatenate(windows, axis=0), ((1,), (0,)))
        grad = products[CH : 2 * CH] + shifted(products[:CH], 1) + shifted(products[2 * CH :], -1)
        n = normed[h]
        sigma = sigmoid(n)
        grad = grad * sigma * (1.0 + n * (1.0 - sigma))
        inner = jnp.sum(grad * n, axis=0, keepdims=True) * (1.0 / CH)
        result = scale[h] * (grad - n * inner) + mine[CH : 2 * CH].astype(F32)
        results.append(result.astype(BF16))
    placed = dot(row_major().astype(F32).T.astype(BF16), jnp.concatenate(results, axis=0), ((1,), (0,)))
    for f in range(F):
        grad_out[f] = placed[:, f * W : (f + 1) * W].astype(BF16)
    done[...] = jnp.zeros(done.shape, F32)


def sum_kernel(parts, *refs):
    out = refs[-1]
    total = parts[0].astype(F32)
    for i in range(1, parts.shape[0]):
        total = total + parts[i].astype(F32)
    total = total.astype(BF16)
    for i in range(out.shape[0]):
        out[i] = total


def unpack_kernel(norm_factor, packed, out, held, sems):
    copies = []
    blocks = [
        jnp.concatenate([packed[half, j * TILE : (j + 1) * TILE, :].astype(F32) for j in range(TILES)], axis=1)
        * norm_factor
        for half in range(2)
    ]
    for t in range(3):
        for c in range(3):
            for half in range(2):
                column = blocks[half][:, (t * 3 + c) * CH : (t * 3 + c + 1) * CH]
                for k in range(3):
                    held[t * 9 + (2 - k) * 3 + c, half * HALF : (half + 1) * HALF] = column[k * HALF : (k + 1) * HALF]
        copies.append(pltpu.make_async_copy(held.at[pl.ds(t * 9, 9)], out.at[pl.ds(t * 9, 9)], sems.at[t]))
        copies[-1].start()
    for copy in copies:
        copy.wait()


def call(kernel, name, outs, args, flops=0, smem=(), after=(), out_hbm=(), scratch=(), aliases={}):
    vmem, anywhere = pl.BlockSpec(memory_space=pltpu.VMEM), pl.BlockSpec(memory_space=pl.ANY)
    return pl.pallas_call(
        kernel,
        out_shape=tuple(jax.ShapeDtypeStruct(shape, dtype) for shape, dtype in outs),
        in_specs=[pl.BlockSpec(memory_space=pltpu.SMEM)] * len(smem) + [vmem] * len(args) + [anywhere] * len(after),
        out_specs=tuple(anywhere if i in out_hbm else vmem for i in range(len(outs))),
        scratch_shapes=scratch,
        input_output_aliases=aliases,
        compiler_params=pltpu.CompilerParams(vmem_limit_bytes=16 << 20),
        cost_estimate=pl.CostEstimate(flops=flops, bytes_accessed=0, transcendentals=0),
        name=name,
    )(*smem, *args, *after)


def sum_to_slots(parts, count, name, after=()):
    return call(sum_kernel, name, [((count,) + parts.shape[1:], BF16)], (parts,), after=after)[0]


def turned(count, first):
    return [[(i + first) % count for i in range(count)]]


def local(features, weights, cotangent):
    tm, rows = lax.axis_size(TM), lax.axis_size(ROWS)
    near, depth = lax.axis_size(NEAR), lax.axis_size("z_pair")
    cells = F * tm * H * rows * W
    features = features.reshape(F, CH * H, W)
    cotangent = cotangent.reshape(F, CH * H, W)

    forward, back = [(i, i + 1) for i in range(tm - 1)], [(i + 1, i) for i in range(tm - 1)]
    last_frames, features, cotangent = call(
        load_kernel,
        "load",
        [((2, CH * H, W), BF16), ((F, CH * H, W), BF16), ((F, CH * H, W), BF16)],
        (),
        after=[pltpu.with_memory_space_constraint(value, pltpu.HBM) for value in (features, cotangent)],
        scratch=[pltpu.SemaphoreType.DMA((3,))],
    )
    before = lax.ppermute(last_frames, TM, forward)
    own, bottom, top, order = call(
        cot_kernel,
        "cot_rows",
        [((H * CH, FW), BF16), ((CH, FW), BF16), ((CH, FW), BF16), ((H * CH, H * CH), BF16)],
        (cotangent,),
        1 << 33,
    )
    above = lax.ppermute(bottom, ROWS, [(i, i + 1) for i in range(rows - 1)])
    below = lax.ppermute(top, ROWS, [(i + 1, i) for i in range(rows - 1)])
    act, normed, scale = call(
        active_kernel,
        "active",
        [((H, TAP, FW), BF16), ((H, CH, FW), F32), ((H, 1, FW), F32)],
        (features, order),
    )
    (wsum,) = call(inner_kernel, "own_cells", [((TAP, 3 * TAP), F32)], (own, act))
    wsum, past_act = call(
        past_kernel,
        "frames_before",
        [((TAP, 3 * TAP), F32), ((2, TAP, NEXT), BF16)],
        (before, own, order, wsum),
    )
    core = lax.axis_index("core").astype(jnp.int32).reshape(1)
    kept, given, first_frames = call(
        edge_kernel,
        "edge_rows",
        [((PACKED, W), F32), ((PACKED, W), BF16), (((H + 2) * CH, NEXT), BF16)],
        (above, below, own, act, past_act, wsum),
        smem=(core,),
        scratch=[pltpu.VMEM((TAP, TILES * W), F32)],
    )
    exchanged = lax.all_gather(given, "core")
    later = lax.ppermute(first_frames, TM, back)
    input_grad, done = call(
        input_kernel,
        "input_grad",
        [((F, CH * H, W), BF16), ((8, W), F32)],
        (above, below, own, later, normed, scale, weights.reshape(27, CH, CH)),
        1 << 31,
    )

    (packed,) = call(add_kernel, "core_sum", [((PACKED, W), BF16)], (kept, exchanged), smem=(core,))
    parts = lax.all_to_all(packed.reshape(near, PACKED // near, W), NEAR, 0, 0, axis_index_groups=turned(near, 24))
    slabs = sum_to_slots(parts, depth, "plane_sum")
    slabs = lax.all_to_all(slabs, "z_pair", 0, 0, axis_index_groups=turned(depth, 4))
    slots = sum_to_slots(slabs, near, "depth_sum", after=(done,))
    own_half = lax.all_to_all(slots, NEAR, 0, 0, axis_index_groups=turned(near, 24)).reshape(PACKED, W)
    whole = lax.all_gather(own_half, "core")
    (weight_grad,) = call(
        lambda *refs: unpack_kernel(1.0 / float(cells) ** 0.5, *refs),
        "unpack",
        [((27, CH, CH), F32)],
        (whole,),
        out_hbm=(0,),
        scratch=[pltpu.VMEM((27, CH, CH), F32), pltpu.SemaphoreType.DMA((3,))],
    )
    return (input_grad.reshape(F, CH, H, W), weight_grad.reshape(3, 3, 3, CH, CH))


def solution(mesh):
    fine = Mesh(
        mesh.devices.reshape(2, 4, 2, 2, 8, 2), ("y_hi", "x", "core", "y_lo", "z_pair", "z_in")
    )
    return jax.shard_map(
        local,
        mesh=fine,
        in_specs=(P(TM, None, ROWS, None), P(), P(TM, None, ROWS, None)),
        out_specs=(P(TM, None, ROWS, None), P()),
        check_vma=False,
    )
```

```python
import jax
import jax.numpy as jnp
from jax import lax
from jax.experimental import pallas as pl
from jax.experimental.pallas import tpu as pltpu
from jax.sharding import Mesh, PartitionSpec as P

TM = ("y_hi", "x", "core")
ROWS = ("y_lo", "z_pair", "z_in")
NEAR = ("y_hi", "x", "y_lo", "z_in")
CH = 96
W = 128
F = 4
H = 4
FW = F * W
NEXT = 2 * W
TAP = 3 * CH
HALF = CH // 2
TILE = 3 * HALF
TILES = 7
PACKED = 1024
F32 = jnp.float32
BF16 = jnp.bfloat16


def dot(a, b, contract):
    return lax.dot_general(a, b, (contract, ((), ())), preferred_element_type=F32)


def row_major():
    parts = []
    for h in range(H):
        pair = lax.broadcasted_iota(jnp.int32, (CH, H * CH), 1)
        channel = lax.broadcasted_iota(jnp.int32, (CH, H * CH), 0)
        parts.append(jnp.where(pair == channel * H + h, 1.0, 0.0).astype(BF16))
    return jnp.concatenate(parts, axis=0)


def frames(ref, count):
    return jnp.concatenate([ref[f] for f in range(count)], axis=1)


def shifted(value, step):
    lane = lax.broadcasted_iota(jnp.int32, (CH, W), 1)
    parts = []
    for f in range(value.shape[1] // W):
        part = pltpu.roll(value[:, f * W : (f + 1) * W], (-step) % W, 1)
        parts.append(jnp.where(lane == (W - 1 if step > 0 else 0), 0.0, part))
    return jnp.concatenate(parts, axis=1)


def column_taps(active):
    wide = active.astype(F32)
    return jnp.concatenate([shifted(wide, -1).astype(BF16), active, shifted(wide, 1).astype(BF16)], axis=0)


def time_taps(past, active):
    return jnp.concatenate(
        [
            jnp.concatenate([past, active[:, : FW - NEXT]], axis=1),
            jnp.concatenate([past[:, W:], active[:, : FW - W]], axis=1),
            active,
        ],
        axis=0,
    )


def rows_of(ref, first, count):
    return ref[first * CH : (first + count) * CH, :]


def normalize(x):
    scale = lax.rsqrt(jnp.sum(x * x, axis=0, keepdims=True) * (1.0 / CH) + 1e-06)
    return x * scale, scale


def sigmoid(x):
    return 1.0 / (1.0 + jnp.exp(-x))


def load_kernel(feat_in, cot_in, last_frames, feat, cot, order, sems):
    copies = [
        pltpu.make_async_copy(feat_in.at[pl.ds(F - 2, 2)], last_frames, sems.at[0]),
        pltpu.make_async_copy(cot_in, cot, sems.at[1]),
        pltpu.make_async_copy(feat_in, feat, sems.at[2]),
    ]
    for copy in copies:
        copy.start()
    order[...] = row_major()
    for copy in copies:
        copy.wait()


def cot_kernel(cot, order, own, bottom, top):
    rows = dot(order[...], frames(cot, F), ((1,), (0,))).astype(BF16)
    own[...] = rows
    top[...] = rows[:CH]
    bottom[...] = rows[(H - 1) * CH :]


def active_kernel(feat, order, act, normed, scale):
    values = dot(order[...], frames(feat, F), ((1,), (0,)))
    for h in range(H):
        n, scale[h] = normalize(values[h * CH : (h + 1) * CH])
        normed[h] = n
        act[h] = column_taps((n * sigmoid(n)).astype(BF16))


def inner_kernel(own, act, wsum):
    def term(first, count, h):
        past = jnp.zeros((TAP, NEXT), BF16)
        return dot(rows_of(own, first, count), time_taps(past, act[h]), ((1,), (1,)))

    both = term(0, 3, 1) + term(1, 3, 2)
    first, last = term(0, 2, 0), term(2, 2, 3)
    wsum[:CH, :] = both[:CH] + last[:CH]
    wsum[CH : 2 * CH, :] = both[CH : 2 * CH] + first[:CH] + last[CH:]
    wsum[2 * CH :, :] = both[2 * CH :] + first[CH:]


def past_kernel(before, own, order, early, past_act):
    values = dot(order[...], frames(before, 2), ((1,), (0,)))
    terms = []
    for h in range(H):
        n, _ = normalize(values[h * CH : (h + 1) * CH])
        past = column_taps((n * sigmoid(n)).astype(BF16))
        if h in (0, H - 1):
            past_act[h // (H - 1)] = past
        late = jnp.concatenate([past[:, W:], jnp.zeros((TAP, W), BF16)], axis=1)
        rows = rows_of(own, max(h - 1, 0), 3 - (h in (0, H - 1)))
        terms.append(dot(rows[:, :NEXT], jnp.concatenate([past, late], axis=0), ((1,), (1,))))
    first, second, third, last = terms
    both = second + third
    early[:CH, :] = both[:CH] + last[:CH]
    early[CH : 2 * CH, :] = both[CH : 2 * CH] + first[:CH] + last[CH:]
    early[2 * CH :, :] = both[2 * CH :] + first[CH:]


def above_kernel(above, act, past_act, wsum, early, total):
    term = dot(above[...], time_taps(past_act[0], act[0]), ((1,), (1,)))
    for k in range(3):
        rows = slice(k * CH, (k + 1) * CH)
        soon, late = wsum[rows, : 2 * TAP] + early[rows], wsum[rows, 2 * TAP :]
        if k == 0:
            soon, late = soon + term[:, : 2 * TAP], late + term[:, 2 * TAP :]
        total[rows, : 2 * TAP] = soon
        total[rows, 2 * TAP : 3 * TAP] = late
        total[rows, 3 * TAP :] = jnp.zeros((CH, TILES * W - 3 * TAP), F32)


def below_kernel(core, above, below, own, act, past_act, total, kept, given, first_frames, last):
    lower = below[...]
    last[:, : 3 * TAP] = total[2 * CH :, : 3 * TAP] + dot(lower, time_taps(past_act[1], act[H - 1]), ((1,), (1,)))
    last[:, 3 * TAP :] = jnp.zeros((CH, TILES * W - 3 * TAP), F32)
    first_frames[:CH, :] = above[:, :NEXT]
    first_frames[CH : 5 * CH, :] = own[:, :NEXT]
    first_frames[5 * CH :, :] = lower[:, :NEXT]
    for out, half in ((given, 1 - core[0]), (kept, core[0])):
        for k in range(3):
            source, first = (last, 0) if k == 2 else (total, k * CH)
            rows = pl.ds(pl.multiple_of(first + half * HALF, HALF), HALF)
            for j in range(TILES):
                tile = source[rows, j * W : (j + 1) * W]
                out[j * TILE + k * HALF : j * TILE + (k + 1) * HALF, :] = tile.astype(out.dtype)
        out[TILES * TILE :, :] = jnp.zeros((PACKED - TILES * TILE, W), out.dtype)


def add_kernel(core, kept, exchanged, out):
    out[...] = (kept[...] + exchanged[1 - core[0]].astype(F32)).astype(BF16)


def input_kernel(above, below, own, later, normed, scale, weights, grad_out, done):
    stacked = [
        jnp.concatenate([weights[t * 9 + (2 - k) * 3 + c].astype(F32) for c in range(3)], axis=1)
        for t in range(3)
        for k in range(3)
    ]
    by_out = jnp.concatenate(stacked, axis=0).T.astype(BF16)
    rows = jnp.concatenate([above[...], own[...], below[...]], axis=0)
    results = []
    for h in range(H):
        mine, ahead = rows[h * CH : (h + 3) * CH], rows_of(later, h, 3)
        windows = [
            jnp.concatenate([mine[:, (2 - t) * W :], ahead[:, : (2 - t) * W]], axis=1) if t < 2 else mine
            for t in range(3)
        ]
        products = dot(by_out, jnp.concatenate(windows, axis=0), ((1,), (0,)))
        grad = products[CH : 2 * CH] + shifted(products[:CH], 1) + shifted(products[2 * CH :], -1)
        n = normed[h]
        sigma = sigmoid(n)
        grad = grad * sigma * (1.0 + n * (1.0 - sigma))
        inner = jnp.sum(grad * n, axis=0, keepdims=True) * (1.0 / CH)
        result = scale[h] * (grad - n * inner) + mine[CH : 2 * CH].astype(F32)
        results.append(result.astype(BF16))
    placed = dot(row_major().astype(F32).T.astype(BF16), jnp.concatenate(results, axis=0), ((1,), (0,)))
    for f in range(F):
        grad_out[f] = placed[:, f * W : (f + 1) * W].astype(BF16)
    done[...] = jnp.zeros(done.shape, F32)


def sum_kernel(parts, *refs):
    out = refs[-1]
    total = parts[0].astype(F32)
    for i in range(1, parts.shape[0]):
        total = total + parts[i].astype(F32)
    total = total.astype(BF16)
    for i in range(out.shape[0]):
        out[i] = total


def unpack_kernel(norm_factor, packed, out, held, sems):
    copies = []
    blocks = [
        jnp.concatenate([packed[half, j * TILE : (j + 1) * TILE, :].astype(F32) for j in range(TILES)], axis=1)
        * norm_factor
        for half in range(2)
    ]
    for t in range(3):
        for c in range(3):
            for half in range(2):
                column = blocks[half][:, (t * 3 + c) * CH : (t * 3 + c + 1) * CH]
                for k in range(3):
                    held[t * 9 + (2 - k) * 3 + c, half * HALF : (half + 1) * HALF] = column[k * HALF : (k + 1) * HALF]
        copies.append(pltpu.make_async_copy(held.at[pl.ds(t * 9, 9)], out.at[pl.ds(t * 9, 9)], sems.at[t]))
        copies[-1].start()
    for copy in copies:
        copy.wait()


def call(kernel, name, outs, args, flops=0, smem=(), after=(), out_hbm=(), scratch=(), aliases={}):
    vmem, anywhere = pl.BlockSpec(memory_space=pltpu.VMEM), pl.BlockSpec(memory_space=pl.ANY)
    return pl.pallas_call(
        kernel,
        out_shape=tuple(jax.ShapeDtypeStruct(shape, dtype) for shape, dtype in outs),
        in_specs=[pl.BlockSpec(memory_space=pltpu.SMEM)] * len(smem) + [vmem] * len(args) + [anywhere] * len(after),
        out_specs=tuple(anywhere if i in out_hbm else vmem for i in range(len(outs))),
        scratch_shapes=scratch,
        input_output_aliases=aliases,
        compiler_params=pltpu.CompilerParams(vmem_limit_bytes=16 << 20),
        cost_estimate=pl.CostEstimate(flops=flops, bytes_accessed=0, transcendentals=0),
        name=name,
    )(*smem, *args, *after)


def sum_to_slots(parts, count, name, after=()):
    return call(sum_kernel, name, [((count,) + parts.shape[1:], BF16)], (parts,), after=after)[0]


def turned(count, first):
    return [[(i + first) % count for i in range(count)]]


def local(features, weights, cotangent):
    tm, rows = lax.axis_size(TM), lax.axis_size(ROWS)
    near, depth = lax.axis_size(NEAR), lax.axis_size("z_pair")
    cells = F * tm * H * rows * W
    features = features.reshape(F, CH * H, W)
    cotangent = cotangent.reshape(F, CH * H, W)

    forward, back = [(i, i + 1) for i in range(tm - 1)], [(i + 1, i) for i in range(tm - 1)]
    last_frames, features, cotangent, order = call(
        load_kernel,
        "load",
        [((2, CH * H, W), BF16), ((F, CH * H, W), BF16), ((F, CH * H, W), BF16), ((H * CH, H * CH), BF16)],
        (),
        after=[pltpu.with_memory_space_constraint(value, pltpu.HBM) for value in (features, cotangent)],
        scratch=[pltpu.SemaphoreType.DMA((3,))],
    )
    before = lax.ppermute(last_frames, TM, forward)
    own, bottom, top = call(
        cot_kernel,
        "cot_rows",
        [((H * CH, FW), BF16), ((CH, FW), BF16), ((CH, FW), BF16)],
        (cotangent, order),
        1 << 33,
    )
    above = lax.ppermute(bottom, ROWS, [(i, i + 1) for i in range(rows - 1)])
    below = lax.ppermute(top, ROWS, [(i + 1, i) for i in range(rows - 1)])
    act, normed, scale = call(
        active_kernel,
        "active",
        [((H, TAP, FW), BF16), ((H, CH, FW), F32), ((H, 1, FW), F32)],
        (features, order),
    )
    (wsum,) = call(inner_kernel, "own_cells", [((TAP, 3 * TAP), F32)], (own, act))
    early, past_act = call(
        past_kernel,
        "frames_before",
        [((TAP, 2 * TAP), F32), ((2, TAP, NEXT), BF16)],
        (before, own, order),
    )
    core = lax.axis_index("core").astype(jnp.int32).reshape(1)
    (total,) = call(
        above_kernel, "row_above", [((TAP, TILES * W), F32)], (above, act, past_act, wsum, early)
    )
    kept, given, first_frames = call(
        below_kernel,
        "row_below",
        [((PACKED, W), F32), ((PACKED, W), BF16), (((H + 2) * CH, NEXT), BF16)],
        (above, below, own, act, past_act, total),
        smem=(core,),
        scratch=[pltpu.VMEM((CH, TILES * W), F32)],
    )
    exchanged = lax.all_gather(given, "core")
    later = lax.ppermute(first_frames, TM, back)
    input_grad, done = call(
        input_kernel,
        "input_grad",
        [((F, CH * H, W), BF16), ((8, W), F32)],
        (above, below, own, later, normed, scale, weights.reshape(27, CH, CH)),
        1 << 31,
    )

    (packed,) = call(add_kernel, "core_sum", [((PACKED, W), BF16)], (kept, exchanged), smem=(core,))
    parts = lax.all_to_all(packed.reshape(near, PACKED // near, W), NEAR, 0, 0, axis_index_groups=turned(near, 24))
    slabs = sum_to_slots(parts, depth, "plane_sum")
    slabs = lax.all_to_all(slabs, "z_pair", 0, 0, axis_index_groups=turned(depth, 4))
    slots = sum_to_slots(slabs, near, "depth_sum", after=(done,))
    own_half = lax.all_to_all(slots, NEAR, 0, 0, axis_index_groups=turned(near, 24)).reshape(PACKED, W)
    whole = lax.all_gather(own_half, "core")
    (weight_grad,) = call(
        lambda *refs: unpack_kernel(1.0 / float(cells) ** 0.5, *refs),
        "unpack",
        [((27, CH, CH), F32)],
        (whole,),
        out_hbm=(0,),
        scratch=[pltpu.VMEM((27, CH, CH), F32), pltpu.SemaphoreType.DMA((3,))],
    )
    return (input_grad.reshape(F, CH, H, W), weight_grad.reshape(3, 3, 3, CH, CH))


def solution(mesh):
    fine = Mesh(
        mesh.devices.reshape(2, 4, 2, 2, 8, 2), ("y_hi", "x", "core", "y_lo", "z_pair", "z_in")
    )
    return jax.shard_map(
        local,
        mesh=fine,
        in_specs=(P(TM, None, ROWS, None), P(), P(TM, None, ROWS, None)),
        out_specs=(P(TM, None, ROWS, None), P()),
        check_vma=False,
    )
```

```python
import jax
import jax.numpy as jnp
from jax import lax
from jax.experimental import pallas as pl
from jax.experimental.pallas import tpu as pltpu
from jax.sharding import Mesh, PartitionSpec as P

TM = ("y_hi", "x", "core")
ROWS = ("y_lo", "z_pair", "z_in")
NEAR = ("y_hi", "x", "y_lo", "z_in")
CH = 96
W = 128
F = 4
H = 4
FW = F * W
NEXT = 2 * W
TAP = 3 * CH
HALF = CH // 2
TILE = 3 * HALF
TILES = 7
PACKED = 1024
F32 = jnp.float32
BF16 = jnp.bfloat16


def dot(a, b, contract):
    return lax.dot_general(a, b, (contract, ((), ())), preferred_element_type=F32)


def row_major():
    parts = []
    for h in range(H):
        pair = lax.broadcasted_iota(jnp.int32, (CH, H * CH), 1)
        channel = lax.broadcasted_iota(jnp.int32, (CH, H * CH), 0)
        parts.append(jnp.where(pair == channel * H + h, 1.0, 0.0).astype(BF16))
    return jnp.concatenate(parts, axis=0)


def frames(ref, count):
    return jnp.concatenate([ref[f] for f in range(count)], axis=1)


def shifted(value, step):
    lane = lax.broadcasted_iota(jnp.int32, (CH, W), 1)
    parts = []
    for f in range(value.shape[1] // W):
        part = pltpu.roll(value[:, f * W : (f + 1) * W], (-step) % W, 1)
        parts.append(jnp.where(lane == (W - 1 if step > 0 else 0), 0.0, part))
    return jnp.concatenate(parts, axis=1)


def column_taps(active):
    wide = active.astype(F32)
    return jnp.concatenate([shifted(wide, -1).astype(BF16), active, shifted(wide, 1).astype(BF16)], axis=0)


def time_taps(past, active):
    return jnp.concatenate(
        [
            jnp.concatenate([past, active[:, : FW - NEXT]], axis=1),
            jnp.concatenate([past[:, W:], active[:, : FW - W]], axis=1),
            active,
        ],
        axis=0,
    )


def rows_of(ref, first, count):
    return ref[first * CH : (first + count) * CH, :]


def normalize(x):
    scale = lax.rsqrt(jnp.sum(x * x, axis=0, keepdims=True) * (1.0 / CH) + 1e-06)
    return x * scale, scale


def sigmoid(x):
    return 1.0 / (1.0 + jnp.exp(-x))


def load_kernel(feat_in, cot_in, last_frames, feat, cot, sems):
    copies = [
        pltpu.make_async_copy(feat_in.at[pl.ds(F - 2, 2)], last_frames, sems.at[0]),
        pltpu.make_async_copy(cot_in, cot, sems.at[1]),
        pltpu.make_async_copy(feat_in, feat, sems.at[2]),
    ]
    for copy in copies:
        copy.start()
    for copy in copies:
        copy.wait()


def cot_kernel(cot, own, bottom, top, order):
    order[...] = row_major()
    rows = dot(order[...], frames(cot, F), ((1,), (0,))).astype(BF16)
    own[...] = rows
    top[...] = rows[:CH]
    bottom[...] = rows[(H - 1) * CH :]


def active_kernel(feat, order, act, normed, scale):
    values = dot(order[...], frames(feat, F), ((1,), (0,)))
    for h in range(H):
        n, scale[h] = normalize(values[h * CH : (h + 1) * CH])
        normed[h] = n
        act[h] = column_taps((n * sigmoid(n)).astype(BF16))


def inner_kernel(own, act, wsum):
    def term(first, count, h):
        past = jnp.zeros((TAP, NEXT), BF16)
        return dot(rows_of(own, first, count), time_taps(past, act[h]), ((1,), (1,)))

    both = term(0, 3, 1) + term(1, 3, 2)
    first, last = term(0, 2, 0), term(2, 2, 3)
    wsum[:CH, :] = both[:CH] + last[:CH]
    wsum[CH : 2 * CH, :] = both[CH : 2 * CH] + first[:CH] + last[CH:]
    wsum[2 * CH :, :] = both[2 * CH :] + first[CH:]


def past_kernel(before, own, order, inner_sum, wsum, past_act):
    values = dot(order[...], frames(before, 2), ((1,), (0,)))
    zeros = jnp.zeros((CH, 2 * TAP), F32)
    early = jnp.zeros((TAP, 2 * TAP), F32)
    for h in range(H):
        n, _ = normalize(values[h * CH : (h + 1) * CH])
        past = column_taps((n * sigmoid(n)).astype(BF16))
        if h in (0, H - 1):
            past_act[h // (H - 1)] = past
        late = jnp.concatenate([past[:, W:], jnp.zeros((TAP, W), BF16)], axis=1)
        rows = rows_of(own, max(h - 1, 0), 3 - (h in (0, H - 1)))
        term = dot(rows[:, :NEXT], jnp.concatenate([past, late], axis=0), ((1,), (1,)))
        early = early + jnp.concatenate([zeros] * (h == 0) + [term] + [zeros] * (h == H - 1), axis=0)
    wsum[...] = inner_sum[...] + jnp.concatenate([early, jnp.zeros((TAP, TAP), F32)], axis=1)


def edge_kernel(core, above, below, own, act, past_act, wsum, kept, given, first_frames, total):
    upper, lower = above[...], below[...]
    from_above = dot(upper, time_taps(past_act[0], act[0]), ((1,), (1,)))
    from_below = dot(lower, time_taps(past_act[1], act[H - 1]), ((1,), (1,)))
    first_frames[:CH, :] = upper[:, :NEXT]
    first_frames[CH : 5 * CH, :] = own[:, :NEXT]
    first_frames[5 * CH :, :] = lower[:, :NEXT]
    total[:CH, : 3 * TAP] = wsum[:CH] + from_above
    total[CH : 2 * CH, : 3 * TAP] = wsum[CH : 2 * CH]
    total[2 * CH :, : 3 * TAP] = wsum[2 * CH :] + from_below
    total[:, 3 * TAP :] = jnp.zeros((TAP, TILES * W - 3 * TAP), F32)
    for out, half in ((given, 1 - core[0]), (kept, core[0])):
        for k in range(3):
            rows = pl.ds(pl.multiple_of(k * CH + half * HALF, HALF), HALF)
            for j in range(TILES):
                tile = total[rows, j * W : (j + 1) * W]
                out[j * TILE + k * HALF : j * TILE + (k + 1) * HALF, :] = tile.astype(out.dtype)
        out[TILES * TILE :, :] = jnp.zeros((PACKED - TILES * TILE, W), out.dtype)


def add_kernel(core, kept, exchanged, out):
    out[...] = (kept[...] + exchanged[1 - core[0]].astype(F32)).astype(BF16)


def input_kernel(above, below, own, later, normed, scale, weights, grad_out, done):
    stacked = [
        jnp.concatenate([weights[t * 9 + (2 - k) * 3 + c].astype(F32) for c in range(3)], axis=1)
        for t in range(3)
        for k in range(3)
    ]
    by_out = jnp.concatenate(stacked, axis=0).T.astype(BF16)
    rows = jnp.concatenate([above[...], own[...], below[...]], axis=0)
    results = []
    for h in range(H):
        mine, ahead = rows[h * CH : (h + 3) * CH], rows_of(later, h, 3)
        windows = [
            jnp.concatenate([mine[:, (2 - t) * W :], ahead[:, : (2 - t) * W]], axis=1) if t < 2 else mine
            for t in range(3)
        ]
        products = dot(by_out, jnp.concatenate(windows, axis=0), ((1,), (0,)))
        grad = products[CH : 2 * CH] + shifted(products[:CH], 1) + shifted(products[2 * CH :], -1)
        n = normed[h]
        sigma = sigmoid(n)
        grad = grad * sigma * (1.0 + n * (1.0 - sigma))
        inner = jnp.sum(grad * n, axis=0, keepdims=True) * (1.0 / CH)
        result = scale[h] * (grad - n * inner) + mine[CH : 2 * CH].astype(F32)
        results.append(result.astype(BF16))
    placed = dot(row_major().astype(F32).T.astype(BF16), jnp.concatenate(results, axis=0), ((1,), (0,)))
    for f in range(F):
        grad_out[f] = placed[:, f * W : (f + 1) * W].astype(BF16)
    done[...] = jnp.zeros(done.shape, F32)


def sum_kernel(parts, *refs):
    out = refs[-1]
    total = parts[0].astype(F32)
    for i in range(1, parts.shape[0]):
        total = total + parts[i].astype(F32)
    total = total.astype(BF16)
    for i in range(out.shape[0]):
        out[i] = total


def unpack_kernel(norm_factor, packed, out, held, sems):
    copies = []
    blocks = [
        jnp.concatenate([packed[half, j * TILE : (j + 1) * TILE, :].astype(F32) for j in range(TILES)], axis=1)
        * norm_factor
        for half in range(2)
    ]
    for t in range(3):
        for half in range(2):
            for c in range(3):
                column = blocks[half][:, (t * 3 + c) * CH : (t * 3 + c + 1) * CH]
                for k in range(3):
                    held[t * 9 + (2 - k) * 3 + c, half * HALF : (half + 1) * HALF] = column[k * HALF : (k + 1) * HALF]
            place = (pl.ds(t * 9, 9), pl.ds(half * HALF, HALF))
            copies.append(pltpu.make_async_copy(held.at[place], out.at[place], sems.at[2 * t + half]))
            copies[-1].start()
    for copy in copies:
        copy.wait()


def call(kernel, name, outs, args, flops=0, smem=(), after=(), out_hbm=(), scratch=(), aliases={}):
    vmem, anywhere = pl.BlockSpec(memory_space=pltpu.VMEM), pl.BlockSpec(memory_space=pl.ANY)
    return pl.pallas_call(
        kernel,
        out_shape=tuple(jax.ShapeDtypeStruct(shape, dtype) for shape, dtype in outs),
        in_specs=[pl.BlockSpec(memory_space=pltpu.SMEM)] * len(smem) + [vmem] * len(args) + [anywhere] * len(after),
        out_specs=tuple(anywhere if i in out_hbm else vmem for i in range(len(outs))),
        scratch_shapes=scratch,
        input_output_aliases=aliases,
        compiler_params=pltpu.CompilerParams(vmem_limit_bytes=16 << 20),
        cost_estimate=pl.CostEstimate(flops=flops, bytes_accessed=0, transcendentals=0),
        name=name,
    )(*smem, *args, *after)


def sum_to_slots(parts, count, name, after=()):
    return call(sum_kernel, name, [((count,) + parts.shape[1:], BF16)], (parts,), after=after)[0]


def turned(count, first):
    return [[(i + first) % count for i in range(count)]]


def local(features, weights, cotangent):
    tm, rows = lax.axis_size(TM), lax.axis_size(ROWS)
    near, depth = lax.axis_size(NEAR), lax.axis_size("z_pair")
    cells = F * tm * H * rows * W
    features = features.reshape(F, CH * H, W)
    cotangent = cotangent.reshape(F, CH * H, W)

    forward, back = [(i, i + 1) for i in range(tm - 1)], [(i + 1, i) for i in range(tm - 1)]
    last_frames, features, cotangent = call(
        load_kernel,
        "load",
        [((2, CH * H, W), BF16), ((F, CH * H, W), BF16), ((F, CH * H, W), BF16)],
        (),
        after=[pltpu.with_memory_space_constraint(value, pltpu.HBM) for value in (features, cotangent)],
        scratch=[pltpu.SemaphoreType.DMA((3,))],
    )
    before = lax.ppermute(last_frames, TM, forward)
    own, bottom, top, order = call(
        cot_kernel,
        "cot_rows",
        [((H * CH, FW), BF16), ((CH, FW), BF16), ((CH, FW), BF16), ((H * CH, H * CH), BF16)],
        (cotangent,),
        1 << 33,
    )
    above = lax.ppermute(bottom, ROWS, [(i, i + 1) for i in range(rows - 1)])
    below = lax.ppermute(top, ROWS, [(i + 1, i) for i in range(rows - 1)])
    act, normed, scale = call(
        active_kernel,
        "active",
        [((H, TAP, FW), BF16), ((H, CH, FW), F32), ((H, 1, FW), F32)],
        (features, order),
    )
    (wsum,) = call(inner_kernel, "own_cells", [((TAP, 3 * TAP), F32)], (own, act))
    wsum, past_act = call(
        past_kernel,
        "frames_before",
        [((TAP, 3 * TAP), F32), ((2, TAP, NEXT), BF16)],
        (before, own, order, wsum),
    )
    core = lax.axis_index("core").astype(jnp.int32).reshape(1)
    kept, given, first_frames = call(
        edge_kernel,
        "edge_rows",
        [((PACKED, W), F32), ((PACKED, W), BF16), (((H + 2) * CH, NEXT), BF16)],
        (above, below, own, act, past_act, wsum),
        smem=(core,),
        scratch=[pltpu.VMEM((TAP, TILES * W), F32)],
    )
    exchanged = lax.all_gather(given, "core")
    later = lax.ppermute(first_frames, TM, back)
    input_grad, done = call(
        input_kernel,
        "input_grad",
        [((F, CH * H, W), BF16), ((8, W), F32)],
        (above, below, own, later, normed, scale, weights.reshape(27, CH, CH)),
        1 << 31,
    )

    (packed,) = call(add_kernel, "core_sum", [((PACKED, W), BF16)], (kept, exchanged), smem=(core,))
    parts = lax.all_to_all(packed.reshape(near, PACKED // near, W), NEAR, 0, 0, axis_index_groups=turned(near, 24))
    slabs = sum_to_slots(parts, depth, "plane_sum")
    slabs = lax.all_to_all(slabs, "z_pair", 0, 0, axis_index_groups=turned(depth, 4))
    slots = sum_to_slots(slabs, near, "depth_sum", after=(done,))
    own_half = lax.all_to_all(slots, NEAR, 0, 0, axis_index_groups=turned(near, 24)).reshape(PACKED, W)
    whole = lax.all_gather(own_half, "core")
    (weight_grad,) = call(
        lambda *refs: unpack_kernel(1.0 / float(cells) ** 0.5, *refs),
        "unpack",
        [((27, CH, CH), F32)],
        (whole,),
        out_hbm=(0,),
        scratch=[pltpu.VMEM((27, CH, CH), F32), pltpu.SemaphoreType.DMA((6,))],
    )
    return (input_grad.reshape(F, CH, H, W), weight_grad.reshape(3, 3, 3, CH, CH))


def solution(mesh):
    fine = Mesh(
        mesh.devices.reshape(2, 4, 2, 2, 8, 2), ("y_hi", "x", "core", "y_lo", "z_pair", "z_in")
    )
    return jax.shard_map(
        local,
        mesh=fine,
        in_specs=(P(TM, None, ROWS, None), P(), P(TM, None, ROWS, None)),
        out_specs=(P(TM, None, ROWS, None), P()),
        check_vma=False,
    )
```

```python
import jax
import jax.numpy as jnp
from jax import lax
from jax.experimental import pallas as pl
from jax.experimental.pallas import tpu as pltpu
from jax.sharding import Mesh, PartitionSpec as P

TM = ("y_hi", "x", "core")
ROWS = ("y_lo", "z_pair", "z_in")
NEAR = ("z_in", "y_hi", "x", "y_lo")
CH = 96
W = 128
F = 4
H = 4
FW = F * W
NEXT = 2 * W
TAP = 3 * CH
HALF = CH // 2
TILE = 3 * HALF
TILES = 7
PACKED = 1024
F32 = jnp.float32
BF16 = jnp.bfloat16


def dot(a, b, contract):
    return lax.dot_general(a, b, (contract, ((), ())), preferred_element_type=F32)


def row_major():
    parts = []
    for h in range(H):
        pair = lax.broadcasted_iota(jnp.int32, (CH, H * CH), 1)
        channel = lax.broadcasted_iota(jnp.int32, (CH, H * CH), 0)
        parts.append(jnp.where(pair == channel * H + h, 1.0, 0.0).astype(BF16))
    return jnp.concatenate(parts, axis=0)


def frames(ref, count):
    return jnp.concatenate([ref[f] for f in range(count)], axis=1)


def shifted(value, step):
    lane = lax.broadcasted_iota(jnp.int32, (CH, W), 1)
    parts = []
    for f in range(value.shape[1] // W):
        part = pltpu.roll(value[:, f * W : (f + 1) * W], (-step) % W, 1)
        parts.append(jnp.where(lane == (W - 1 if step > 0 else 0), 0.0, part))
    return jnp.concatenate(parts, axis=1)


def column_taps(active):
    wide = active.astype(F32)
    return jnp.concatenate([shifted(wide, -1).astype(BF16), active, shifted(wide, 1).astype(BF16)], axis=0)


def time_taps(past, active):
    return jnp.concatenate(
        [
            jnp.concatenate([past, active[:, : FW - NEXT]], axis=1),
            jnp.concatenate([past[:, W:], active[:, : FW - W]], axis=1),
            active,
        ],
        axis=0,
    )


def rows_of(ref, first, count):
    return ref[first * CH : (first + count) * CH, :]


def normalize(x):
    scale = lax.rsqrt(jnp.sum(x * x, axis=0, keepdims=True) * (1.0 / CH) + 1e-06)
    return x * scale, scale


def sigmoid(x):
    return 1.0 / (1.0 + jnp.exp(-x))


def load_kernel(feat_in, cot_in, last_frames, feat, cot, sems):
    copies = [
        pltpu.make_async_copy(feat_in.at[pl.ds(F - 2, 2)], last_frames, sems.at[0]),
        pltpu.make_async_copy(cot_in, cot, sems.at[1]),
        pltpu.make_async_copy(feat_in, feat, sems.at[2]),
    ]
    for copy in copies:
        copy.start()
    for copy in copies:
        copy.wait()


def cot_kernel(cot, own, bottom, top, order):
    order[...] = row_major()
    rows = dot(order[...], frames(cot, F), ((1,), (0,))).astype(BF16)
    own[...] = rows
    top[...] = rows[:CH]
    bottom[...] = rows[(H - 1) * CH :]


def active_kernel(feat, order, act, normed, scale):
    values = dot(order[...], frames(feat, F), ((1,), (0,)))
    for h in range(H):
        n, scale[h] = normalize(values[h * CH : (h + 1) * CH])
        normed[h] = n
        act[h] = column_taps((n * sigmoid(n)).astype(BF16))


def inner_kernel(own, act, wsum):
    def term(first, count, h):
        past = jnp.zeros((TAP, NEXT), BF16)
        return dot(rows_of(own, first, count), time_taps(past, act[h]), ((1,), (1,)))

    both = term(0, 3, 1) + term(1, 3, 2)
    first, last = term(0, 2, 0), term(2, 2, 3)
    wsum[:CH, :] = both[:CH] + last[:CH]
    wsum[CH : 2 * CH, :] = both[CH : 2 * CH] + first[:CH] + last[CH:]
    wsum[2 * CH :, :] = both[2 * CH :] + first[CH:]


def past_kernel(before, own, order, inner_sum, wsum, past_act):
    values = dot(order[...], frames(before, 2), ((1,), (0,)))
    zeros = jnp.zeros((CH, 2 * TAP), F32)
    early = jnp.zeros((TAP, 2 * TAP), F32)
    for h in range(H):
        n, _ = normalize(values[h * CH : (h + 1) * CH])
        past = column_taps((n * sigmoid(n)).astype(BF16))
        if h in (0, H - 1):
            past_act[h // (H - 1)] = past
        late = jnp.concatenate([past[:, W:], jnp.zeros((TAP, W), BF16)], axis=1)
        rows = rows_of(own, max(h - 1, 0), 3 - (h in (0, H - 1)))
        term = dot(rows[:, :NEXT], jnp.concatenate([past, late], axis=0), ((1,), (1,)))
        early = early + jnp.concatenate([zeros] * (h == 0) + [term] + [zeros] * (h == H - 1), axis=0)
    wsum[...] = inner_sum[...] + jnp.concatenate([early, jnp.zeros((TAP, TAP), F32)], axis=1)


def edge_kernel(core, above, below, own, act, past_act, wsum, kept, given, first_frames, total):
    upper, lower = above[...], below[...]
    from_above = dot(upper, time_taps(past_act[0], act[0]), ((1,), (1,)))
    from_below = dot(lower, time_taps(past_act[1], act[H - 1]), ((1,), (1,)))
    first_frames[:CH, :] = upper[:, :NEXT]
    first_frames[CH : 5 * CH, :] = own[:, :NEXT]
    first_frames[5 * CH :, :] = lower[:, :NEXT]
    total[:CH, : 3 * TAP] = wsum[:CH] + from_above
    total[CH : 2 * CH, : 3 * TAP] = wsum[CH : 2 * CH]
    total[2 * CH :, : 3 * TAP] = wsum[2 * CH :] + from_below
    total[:, 3 * TAP :] = jnp.zeros((TAP, TILES * W - 3 * TAP), F32)
    for out, half in ((given, 1 - core[0]), (kept, core[0])):
        for k in range(3):
            rows = pl.ds(pl.multiple_of(k * CH + half * HALF, HALF), HALF)
            for j in range(TILES):
                tile = total[rows, j * W : (j + 1) * W]
                out[j * TILE + k * HALF : j * TILE + (k + 1) * HALF, :] = tile.astype(out.dtype)
        out[TILES * TILE :, :] = jnp.zeros((PACKED - TILES * TILE, W), out.dtype)


def add_kernel(core, kept, exchanged, out):
    out[...] = (kept[...] + exchanged[1 - core[0]].astype(F32)).astype(BF16)


def input_kernel(above, below, own, later, normed, scale, weights, grad_out, done):
    stacked = [
        jnp.concatenate([weights[t * 9 + (2 - k) * 3 + c].astype(F32) for c in range(3)], axis=1)
        for t in range(3)
        for k in range(3)
    ]
    by_out = jnp.concatenate(stacked, axis=0).T.astype(BF16)
    rows = jnp.concatenate([above[...], own[...], below[...]], axis=0)
    results = []
    for h in range(H):
        mine, ahead = rows[h * CH : (h + 3) * CH], rows_of(later, h, 3)
        windows = [
            jnp.concatenate([mine[:, (2 - t) * W :], ahead[:, : (2 - t) * W]], axis=1) if t < 2 else mine
            for t in range(3)
        ]
        products = dot(by_out, jnp.concatenate(windows, axis=0), ((1,), (0,)))
        grad = products[CH : 2 * CH] + shifted(products[:CH], 1) + shifted(products[2 * CH :], -1)
        n = normed[h]
        sigma = sigmoid(n)
        grad = grad * sigma * (1.0 + n * (1.0 - sigma))
        inner = jnp.sum(grad * n, axis=0, keepdims=True) * (1.0 / CH)
        result = scale[h] * (grad - n * inner) + mine[CH : 2 * CH].astype(F32)
        results.append(result.astype(BF16))
    placed = dot(row_major().astype(F32).T.astype(BF16), jnp.concatenate(results, axis=0), ((1,), (0,)))
    for f in range(F):
        grad_out[f] = placed[:, f * W : (f + 1) * W].astype(BF16)
    done[...] = jnp.zeros(done.shape, F32)


def sum_kernel(parts, *refs):
    out = refs[-1]
    total = parts[0].astype(F32)
    for i in range(1, parts.shape[0]):
        total = total + parts[i].astype(F32)
    total = total.astype(BF16)
    for i in range(out.shape[0]):
        out[i] = total


def unpack_kernel(norm_factor, packed, out, held, sems):
    copies = []
    blocks = [
        jnp.concatenate([packed[half, j * TILE : (j + 1) * TILE, :].astype(F32) for j in range(TILES)], axis=1)
        * norm_factor
        for half in range(2)
    ]
    for t in range(3):
        for c in range(3):
            for half in range(2):
                column = blocks[half][:, (t * 3 + c) * CH : (t * 3 + c + 1) * CH]
                for k in range(3):
                    held[t * 9 + (2 - k) * 3 + c, half * HALF : (half + 1) * HALF] = column[k * HALF : (k + 1) * HALF]
        copies.append(pltpu.make_async_copy(held.at[pl.ds(t * 9, 9)], out.at[pl.ds(t * 9, 9)], sems.at[t]))
        copies[-1].start()
    for copy in copies:
        copy.wait()


def call(kernel, name, outs, args, flops=0, smem=(), after=(), out_hbm=(), scratch=(), aliases={}):
    vmem, anywhere = pl.BlockSpec(memory_space=pltpu.VMEM), pl.BlockSpec(memory_space=pl.ANY)
    return pl.pallas_call(
        kernel,
        out_shape=tuple(jax.ShapeDtypeStruct(shape, dtype) for shape, dtype in outs),
        in_specs=[pl.BlockSpec(memory_space=pltpu.SMEM)] * len(smem) + [vmem] * len(args) + [anywhere] * len(after),
        out_specs=tuple(anywhere if i in out_hbm else vmem for i in range(len(outs))),
        scratch_shapes=scratch,
        input_output_aliases=aliases,
        compiler_params=pltpu.CompilerParams(vmem_limit_bytes=16 << 20),
        cost_estimate=pl.CostEstimate(flops=flops, bytes_accessed=0, transcendentals=0),
        name=name,
    )(*smem, *args, *after)


def sum_to_slots(parts, count, name, after=()):
    return call(sum_kernel, name, [((count,) + parts.shape[1:], BF16)], (parts,), after=after)[0]


def turned(count, first):
    return [[(i + first) % count for i in range(count)]]


def local(features, weights, cotangent):
    tm, rows = lax.axis_size(TM), lax.axis_size(ROWS)
    near, depth = lax.axis_size(NEAR), lax.axis_size("z_pair")
    cells = F * tm * H * rows * W
    features = features.reshape(F, CH * H, W)
    cotangent = cotangent.reshape(F, CH * H, W)

    forward, back = [(i, i + 1) for i in range(tm - 1)], [(i + 1, i) for i in range(tm - 1)]
    last_frames, features, cotangent = call(
        load_kernel,
        "load",
        [((2, CH * H, W), BF16), ((F, CH * H, W), BF16), ((F, CH * H, W), BF16)],
        (),
        after=[pltpu.with_memory_space_constraint(value, pltpu.HBM) for value in (features, cotangent)],
        scratch=[pltpu.SemaphoreType.DMA((3,))],
    )
    before = lax.ppermute(last_frames, TM, forward)
    own, bottom, top, order = call(
        cot_kernel,
        "cot_rows",
        [((H * CH, FW), BF16), ((CH, FW), BF16), ((CH, FW), BF16), ((H * CH, H * CH), BF16)],
        (cotangent,),
        1 << 33,
    )
    above = lax.ppermute(bottom, ROWS, [(i, i + 1) for i in range(rows - 1)])
    below = lax.ppermute(top, ROWS, [(i + 1, i) for i in range(rows - 1)])
    act, normed, scale = call(
        active_kernel,
        "active",
        [((H, TAP, FW), BF16), ((H, CH, FW), F32), ((H, 1, FW), F32)],
        (features, order),
    )
    (wsum,) = call(inner_kernel, "own_cells", [((TAP, 3 * TAP), F32)], (own, act))
    wsum, past_act = call(
        past_kernel,
        "frames_before",
        [((TAP, 3 * TAP), F32), ((2, TAP, NEXT), BF16)],
        (before, own, order, wsum),
    )
    core = lax.axis_index("core").astype(jnp.int32).reshape(1)
    kept, given, first_frames = call(
        edge_kernel,
        "edge_rows",
        [((PACKED, W), F32), ((PACKED, W), BF16), (((H + 2) * CH, NEXT), BF16)],
        (above, below, own, act, past_act, wsum),
        smem=(core,),
        scratch=[pltpu.VMEM((TAP, TILES * W), F32)],
    )
    exchanged = lax.all_gather(given, "core")
    later = lax.ppermute(first_frames, TM, back)
    input_grad, done = call(
        input_kernel,
        "input_grad",
        [((F, CH * H, W), BF16), ((8, W), F32)],
        (above, below, own, later, normed, scale, weights.reshape(27, CH, CH)),
        1 << 31,
    )

    (packed,) = call(add_kernel, "core_sum", [((PACKED, W), BF16)], (kept, exchanged), smem=(core,))
    parts = lax.all_to_all(packed.reshape(near, PACKED // near, W), NEAR, 0, 0, axis_index_groups=turned(near, 12))
    slabs = sum_to_slots(parts, depth, "plane_sum")
    slabs = lax.all_to_all(slabs, "z_pair", 0, 0, axis_index_groups=turned(depth, 4))
    slots = sum_to_slots(slabs, near, "depth_sum", after=(done,))
    own_half = lax.all_to_all(slots, NEAR, 0, 0, axis_index_groups=turned(near, 12)).reshape(PACKED, W)
    whole = lax.all_gather(own_half, "core")
    (weight_grad,) = call(
        lambda *refs: unpack_kernel(1.0 / float(cells) ** 0.5, *refs),
        "unpack",
        [((27, CH, CH), F32)],
        (whole,),
        out_hbm=(0,),
        scratch=[pltpu.VMEM((27, CH, CH), F32), pltpu.SemaphoreType.DMA((3,))],
    )
    return (input_grad.reshape(F, CH, H, W), weight_grad.reshape(3, 3, 3, CH, CH))


def solution(mesh):
    fine = Mesh(
        mesh.devices.reshape(2, 4, 2, 2, 8, 2), ("y_hi", "x", "core", "y_lo", "z_pair", "z_in")
    )
    return jax.shard_map(
        local,
        mesh=fine,
        in_specs=(P(TM, None, ROWS, None), P(), P(TM, None, ROWS, None)),
        out_specs=(P(TM, None, ROWS, None), P()),
        check_vma=False,
    )
```
